512 devices in a mesh: seq: 64 (over y, z_hi, x), section: 8 (over z_lo, core).
Axes of the slice: x: 4, y: 4, z: 16 (z_hi: 4, z_lo: 4; z = z_hi * 4 + z_lo), core: 2. Of those that a mesh axis runs over, the one named last changes fastest.
Arguments:
- normed_input: bfloat16 [8192, 3584], P('seq', 'section'), may hold values from -6 to 6
- w_down: bfloat16 [3584, 128], P('section'), may hold values from -0.09375 to 0.09375
- query_rows: bfloat16 [8192, 1792], P('seq', 'section'), may hold values from -9 to 9
- key_rows: bfloat16 [8192, 1792], P('seq', 'section'), may hold values from -9 to 9
- value_base: bfloat16 [8192, 1792], P('seq', 'section'), may hold values from -6 to 6
- cotangent: bfloat16 [8192, 1792], P('seq', 'section'), may hold values from -6 to 6
- master: float32 [128, 1792], P('seq', 'section'), may hold values from -5 to 5
- first_moment: float32 [128, 1792], P('seq', 'section'), may hold values from -4 to 4
- second_moment: float32 [128, 1792], P('seq', 'section'), may hold values from 0.1 to 2
Outputs:
- query_grad: bfloat16 [8192, 1792], P('seq', 'section')
- key_grad: bfloat16 [8192, 1792], P('seq', 'section')
- new_master: float32 [128, 1792], P('seq', 'section')
- new_first: float32 [128, 1792], P('seq', 'section')
- new_second: float32 [128, 1792], P('seq', 'section')
The draws below stay inside these ranges and needn't reach their ends.
All inputs are finite; a program needn't handle non-finite values.
Results may differ from the reference program's by a relative error of at most 0.011.
Values may be sent and summed in bfloat16 or wider, within the bound.
No kernel may reach another device: no remote copies, remote signals or barrier semaphores. Data moves between devices by JAX's collectives and lax.ppermute only.
A program may use at most 128 MiB of HBM per device.

```python
import math
import jax
import jax.numpy as jnp
from jax import lax

D = 3584
HEADS = 16
HEAD = 112
RANK = 128
STEP = 2
TOK_DEV = 128
TOKENS = 8192
N_SEQ = 64


def drawn_keys(key):
    return jnp.clip(jax.random.normal(jax.random.fold_in(key, 12), (TOKENS, HEADS * HEAD), jnp.float32), -9.0, 9.0)


def row_number():
    return lax.broadcasted_iota(jnp.int32, (TOKENS, HEADS * HEAD), 0)


def draw_query_rows(key, part):
    first_key = drawn_keys(key)[0:1, :]
    key = jax.random.fold_in(key, 11)
    values = jnp.clip(jax.random.normal(key, (TOKENS, HEADS * HEAD), jnp.float32), -9.0, 9.0)
    factor = math.log(TOKENS) / math.sqrt(HEAD)
    aligned = jnp.clip(factor * (first_key + 0.3 * values), -9.0, 9.0)
    rows = row_number()
    values = jnp.where((rows >= TOKENS - TOK_DEV) & (rows < TOKENS - 1), aligned, values)
    return values.astype(jnp.bfloat16)


def draw_key_rows(key, part):
    values = drawn_keys(key)
    return values.astype(jnp.bfloat16)


def shard_levels(key, dims, cuts, least, top_value):
    def one(position, shards_of):
        heights = jax.random.uniform(jax.random.fold_in(jax.random.fold_in(key, 6), position), (shards_of,), jnp.float32, least / len(cuts), top_value / len(cuts))
        return jnp.repeat(jnp.exp(heights), dims[position] // shards_of).reshape((-1,) + (1,) * (len(dims) - position - 1))

    level = one(*cuts[0])
    for cut in cuts[1:]:
        level = level * one(*cut)
    return level


def scatter_about(rng, shape, width, most, pieces=(), kind=jnp.bfloat16):
    values = width * jax.random.normal(rng, shape, jnp.float32)
    if pieces:
        values = values * shard_levels(rng, shape, pieces, -0.22, 0.18)
    return jnp.clip(values, -most, most).astype(kind)


def setup_inputs(seed: int = 0) -> dict:
    key_of = jax.random.split(jax.random.key(seed), 10)
    normed_input = scatter_about(key_of[0], (TOKENS, D), 1.0, 6.0, ((0, 64), (1, 8)))
    w_down = scatter_about(key_of[1], (D, RANK), D ** -0.5, 0.09375, ((0, 8),))
    query_rows = draw_query_rows(jax.random.fold_in(key_of[9], 71), 0)
    key_rows = draw_key_rows(jax.random.fold_in(key_of[9], 71), 0)
    value_base = scatter_about(key_of[4], (TOKENS, HEADS * HEAD), 1.0, 6.0, ((0, 64), (1, 8)))
    cotangent = scatter_about(key_of[5], (TOKENS, HEADS * HEAD), 1.0, 6.0, ((0, 64), (1, 8)))
    master = scatter_about(key_of[6], (RANK, HEADS * HEAD), 1.0, 5.0, ((0, 64), (1, 8)), jnp.float32)
    first_moment = scatter_about(key_of[7], (RANK, HEADS * HEAD), 0.5, 4.0, ((0, 64), (1, 8)), jnp.float32)
    second_moment = jnp.clip(jnp.exp(math.log(2.0) - 2.9957323 * jax.random.uniform(key_of[8], (RANK, HEADS * HEAD), jnp.float32) ** shard_levels(key_of[8], (RANK, HEADS * HEAD), ((0, 64), (1, 8)), -0.2, 0.2)), 0.1, 2.0)
    return {"normed_input": normed_input, "w_down": w_down, "query_rows": query_rows, "key_rows": key_rows, "value_base": value_base, "cotangent": cotangent, "master": master, "first_moment": first_moment, "second_moment": second_moment}


BETA_ONE = 0.9
BETA_TWO = 0.95
LEARN_RATE = 0.01
WEIGHT_DECAY = 0.1
ADAM_EPSILON = 1e-08
MASK_VALUE = -1e+30

def heads_first(matrix):
    return matrix.reshape(matrix.shape[0], HEADS, HEAD).transpose(1, 0, 2)

def heads_last(stacked):
    return stacked.transpose(1, 0, 2).reshape(stacked.shape[1], HEADS * HEAD)

def head_grads(inputs_pack):
    q_head, k_head, v_head, o_head = inputs_pack
    score_scale = 1.0 / math.sqrt(HEAD)
    key_ids = lax.broadcasted_iota(jnp.int32, (1, TOKENS), 1)

    def one_group(carry, group):
        key_sum, value_sum = carry
        start = (group * TOK_DEV).astype(jnp.int32)
        q_rows = lax.dynamic_slice_in_dim(q_head, start, TOK_DEV, 0)
        o_rows = lax.dynamic_slice_in_dim(o_head, start, TOK_DEV, 0)
        row_ids = start + lax.broadcasted_iota(jnp.int32, (TOK_DEV, 1), 0)
        scores = jnp.dot(q_rows, k_head.T, preferred_element_type=jnp.float32) * score_scale
        scores = jnp.where(key_ids <= row_ids, scores, MASK_VALUE)
        row_max = lax.optimization_barrier(jnp.max(scores, axis=1, keepdims=True))
        log_total = row_max + jnp.log(lax.optimization_barrier(jnp.sum(jnp.exp(scores - row_max), axis=1, keepdims=True)))
        attn_prob = jnp.exp(scores - log_total)
        attn_bf = attn_prob.astype(jnp.bfloat16)
        d_prob = jnp.dot(o_rows, v_head.T, preferred_element_type=jnp.float32)
        row_delta = lax.optimization_barrier(jnp.sum(attn_prob * d_prob, axis=1, keepdims=True))
        d_score = (attn_prob * (d_prob - row_delta)).astype(jnp.bfloat16)
        query_part = (jnp.dot(d_score, k_head, preferred_element_type=jnp.float32) * score_scale).astype(jnp.bfloat16)
        key_part = lax.optimization_barrier((jnp.dot(d_score.T, q_rows, preferred_element_type=jnp.float32) * score_scale).astype(jnp.bfloat16))
        value_part = lax.optimization_barrier(jnp.dot(attn_bf.T, o_rows, preferred_element_type=jnp.float32).astype(jnp.bfloat16))
        return ((key_sum + key_part.astype(jnp.float32), value_sum + value_part.astype(jnp.float32)), query_part)
    start_sums = (jnp.zeros((TOKENS, HEAD), jnp.float32), jnp.zeros((TOKENS, HEAD), jnp.float32))
    sums, query_parts = lax.scan(one_group, start_sums, jnp.arange(N_SEQ, dtype=jnp.int32))
    return (query_parts.reshape(TOKENS, HEAD), sums[0], sums[1])

def reference(normed_input, w_down, query_rows, key_rows, value_base, cotangent, master, first_moment, second_moment):
    inv_rank = 1.0 / math.sqrt(RANK)
    w_up = master.astype(jnp.bfloat16)
    low_rank = jnp.dot(normed_input, w_down, preferred_element_type=jnp.float32).astype(jnp.bfloat16)
    values = (value_base.astype(jnp.float32) + jnp.dot(low_rank, w_up, preferred_element_type=jnp.float32) * inv_rank).astype(jnp.bfloat16)
    query_parts, key_sums, value_sums = lax.map(head_grads, (heads_first(query_rows), heads_first(key_rows), heads_first(values), heads_first(cotangent)))
    query_grad = heads_last(query_parts)
    key_grad = heads_last(key_sums).astype(jnp.bfloat16)
    d_value = heads_last(value_sums).astype(jnp.bfloat16)
    gradient = jnp.dot(low_rank.T, d_value, preferred_element_type=jnp.float32) * inv_rank
    new_first = BETA_ONE * first_moment + (1.0 - BETA_ONE) * gradient
    new_second = BETA_TWO * second_moment + (1.0 - BETA_TWO) * gradient * gradient
    direction = new_first / (1.0 - BETA_ONE ** STEP) / (jnp.sqrt(new_second / (1.0 - BETA_TWO ** STEP)) + ADAM_EPSILON)
    new_master = master - LEARN_RATE * (direction + WEIGHT_DECAY * master)
    return (query_grad, key_grad, new_master, new_first, new_second)
```

```python
import math

import jax
import jax.numpy as jnp
from jax import lax
from jax.experimental import pallas as pl
from jax.experimental.pallas import tpu as pltpu
from jax.sharding import Mesh, PartitionSpec as P

HEAD = 112
LANES = 128
RANK = 128
STEP = 2

BETA_ONE = 0.9
BETA_TWO = 0.95
LEARN_RATE = 0.01
WEIGHT_DECAY = 0.1
ADAM_EPSILON = 1e-08
MASK_VALUE = -1e30
LOW_MAX = -1e20
SCORE_SCALE = 1.0 / math.sqrt(HEAD)
INV_RANK = 1.0 / math.sqrt(RANK)

BF = jnp.bfloat16
F32 = jnp.float32

TOK = 128
HALF = 64
N_Q = 1024
N_K = 2048
Q_STEP = 256
VMEM_LIMIT = 56 * 1024 * 1024

VMEM = pl.BlockSpec(memory_space=pltpu.VMEM)
SMEM = pl.BlockSpec(memory_space=pltpu.SMEM)


def call(kernel, shapes, specs, scratch=()):
    return pl.pallas_call(
        kernel,
        out_shape=[jax.ShapeDtypeStruct(s, d) for s, d in shapes],
        in_specs=specs,
        out_specs=[VMEM] * len(shapes),
        scratch_shapes=list(scratch),
        compiler_params=pltpu.CompilerParams(vmem_limit_bytes=VMEM_LIMIT),
    )


def dot_nt(a, b):
    return lax.dot_general(a, b, (((1,), (1,)), ((), ())), preferred_element_type=F32)


def dot_tn(a, b):
    return lax.dot_general(a, b, (((0,), (0,)), ((), ())), preferred_element_type=F32)


def rank_of(order):
    return (
        (order >> 5) * 32 + (order & 3) * 8 + ((order >> 3) & 3) * 2 + ((order >> 2) & 1)
    )


def pack_kernel(pos, x_ref, wd_ref, q_ref, do_ref, k_ref, vb_ref, part_ref, keep_ref, send_ref):
    core = pos[4]
    part = jnp.dot(x_ref[...], wd_ref[...], preferred_element_type=F32)
    for s in range(8):
        h = s % 2
        part_ref[s] = part[h * HALF : (h + 1) * HALF]
    keep_ref[...] = jnp.zeros_like(keep_ref)
    send_ref[...] = jnp.zeros_like(send_ref)
    own = pl.ds(pl.multiple_of(core * HALF, HALF), HALF)
    other = pl.ds(pl.multiple_of((1 - core) * HALF, HALF), HALF)
    for i, ref in enumerate((q_ref, do_ref, k_ref, vb_ref)):
        for rows, out in ((own, keep_ref), (other, send_ref)):
            tile = ref[rows, :]
            for h in range(2):
                out[h, :, i * LANES : i * LANES + HEAD] = tile[:, h * HEAD : (h + 1) * HEAD]


def route_kernel(pos, part_ref, keep_ref, recv_ref, out_ref):
    core = pos[4]
    total = part_ref[0]
    for s in range(1, 8):
        total = total + part_ref[s]
    src = lax.broadcasted_iota(jnp.int32, (RANK, RANK), 0)
    dst = lax.broadcasted_iota(jnp.int32, (RANK, RANK), 1)
    order = jnp.where(src == rank_of(dst), 1.0, 0.0).astype(BF)
    low = jnp.dot(total.astype(BF), order, preferred_element_type=F32).astype(BF)
    for j in range(4):
        out_ref[j, :, 512:640] = low
    for h in range(2):
        out_ref[core * 2 + h, :, 0:512] = keep_ref[h]
        out_ref[(1 - core) * 2 + h, :, 0:512] = recv_ref[h]


def token_ids(pos):
    y, x, core = pos[0], pos[2], pos[4]
    n = lax.broadcasted_iota(jnp.int32, (1, N_Q), 1)
    q_tok = y * 2048 + ((n >> 6) & 3) * 512 + (n >> 8) * 128 + core * HALF + (n & 63)
    m = lax.broadcasted_iota(jnp.int32, (N_K, 1), 0)
    half = (m >> 10) ^ core
    k_tok = ((m >> 8) & 3) * 2048 + ((m >> 6) & 3) * 512 + x * 128 + half * HALF + (m & 63)
    return q_tok, k_tok


def first_kernel(pos, q_ref, own_ref, other_ref, w_ref, stat_ref, v_ref):
    dst = lax.broadcasted_iota(jnp.int32, (RANK, RANK), 0)
    src = lax.broadcasted_iota(jnp.int32, (RANK, RANK), 1)
    order = jnp.where(src == rank_of(dst), 1.0, 0.0).astype(BF)
    w_up = jnp.dot(order, w_ref[...], preferred_element_type=F32).astype(BF)
    for h, ref in enumerate((own_ref, other_ref)):
        add = jnp.dot(ref[:, 256:384], w_up, preferred_element_type=F32) * INV_RANK
        v_ref[h * 1024 : (h + 1) * 1024] = (ref[:, 128:256].astype(F32) + add).astype(BF)
    q_tok, k_tok = token_ids(pos)
    keys = jnp.concatenate([own_ref[:, 0:128], other_ref[:, 0:128]], axis=0)
    values = v_ref[...]
    for s in range(N_Q // Q_STEP):
        cols = slice(s * Q_STEP, (s + 1) * Q_STEP)
        scores = dot_nt(keys, q_ref[cols, 0:128]) * SCORE_SCALE
        scores = jnp.where(k_tok <= q_tok[:, cols], scores, MASK_VALUE)
        top = jnp.maximum(jnp.max(scores, axis=0, keepdims=True), LOW_MAX)
        weight = jnp.exp(scores - top)
        total = jnp.sum(weight, axis=0, keepdims=True)
        d_prob = dot_nt(values, q_ref[cols, 128:256])
        delta = jnp.sum(weight * d_prob, axis=0, keepdims=True)
        some = total > 0.0
        safe = jnp.where(some, total, 1.0)
        stat_ref[0:1, cols] = jnp.where(some, top + jnp.log(safe), MASK_VALUE)
        stat_ref[1:2, cols] = delta / safe
    stat_ref[2:8, :] = jnp.zeros((6, N_Q), F32)


def second_kernel(pos, q_ref, own_ref, other_ref, v_ref, stat_ref,
                  dq_ref, keep_ref, send_ref, grad_ref, dk_acc, dv_acc):
    q_tok, k_tok = token_ids(pos)
    keys = jnp.concatenate([own_ref[:, 0:128], other_ref[:, 0:128]], axis=0)
    low = jnp.concatenate([own_ref[:, 256:384], other_ref[:, 256:384]], axis=0)
    values = v_ref[...]
    for s in range(N_Q // Q_STEP):
        cols = slice(s * Q_STEP, (s + 1) * Q_STEP)
        lse = [stat_ref[i, 0:1, cols] for i in range(4)]
        top = jnp.maximum(jnp.maximum(lse[0], lse[1]), jnp.maximum(lse[2], lse[3]))
        share = [jnp.exp(l - top) for l in lse]
        total = share[0] + share[1] + share[2] + share[3]
        delta = sum(share[i] * stat_ref[i, 1:2, cols] for i in range(4)) / total
        log_total = top + jnp.log(total)
        queries, cotan = q_ref[cols, 0:128], q_ref[cols, 128:256]
        scores = dot_nt(keys, queries) * SCORE_SCALE
        scores = jnp.where(k_tok <= q_tok[:, cols], scores, MASK_VALUE)
        prob = jnp.exp(scores - log_total)
        d_prob = dot_nt(values, cotan)
        d_score = (prob * (d_prob - delta)).astype(BF)
        d_key = jnp.dot(d_score, queries, preferred_element_type=F32)
        d_val = jnp.dot(prob.astype(BF), cotan, preferred_element_type=F32)
        if s == 0:
            dk_acc[...] = d_key
            dv_acc[...] = d_val
        else:
            dk_acc[...] += d_key
            dv_acc[...] += d_val
        dq_ref[cols, :] = (dot_tn(d_score, keys) * SCORE_SCALE).astype(BF)
    keep_ref[...] = (dk_acc[0:1024] * SCORE_SCALE)
    send_ref[...] = (dk_acc[1024:2048] * SCORE_SCALE).astype(BF)
    grad_ref[...] = dot_tn(low, dv_acc[...].astype(BF)) * INV_RANK


def sums_kernel(dq_ref, dk_ref, grad_ref, out_ref):
    dq = dq_ref[0].astype(F32)
    dk = dk_ref[0].astype(F32)
    for i in range(1, 4):
        dq = dq + dq_ref[i].astype(F32)
        dk = dk + dk_ref[i].astype(F32)
    grad = grad_ref[0]
    for i in range(1, 32):
        grad = grad + grad_ref[i]
    high = grad.astype(BF)
    rest = (grad - high.astype(F32)).astype(BF)
    for z in range(4):
        rows = slice(z * HALF, (z + 1) * HALF)
        out_ref[z, 0:HALF, 0:128] = dq[rows].astype(BF)
        out_ref[z, 0:HALF, 128:256] = dk[rows].astype(BF)
        out_ref[z, HALF : HALF + 16, 0:128] = jnp.broadcast_to(high[z : z + 1], (16, 128))
        out_ref[z, HALF : HALF + 16, 128:256] = jnp.broadcast_to(rest[z : z + 1], (16, 128))


def last_kernel(pos, keep_ref, recv_ref, master_ref, first_ref, second_ref,
                qg_ref, kg_ref, nm_ref, nf_ref, ns_ref):
    core = pos[4]
    for rows, ref in ((core, keep_ref), (1 - core, recv_ref)):
        at = pl.ds(pl.multiple_of(rows * HALF, HALF), HALF)
        for out, lane in ((qg_ref, 0), (kg_ref, 128)):
            tile = jnp.concatenate(
                [ref[h, 0:HALF, lane : lane + HEAD] for h in range(2)], axis=1
            )
            out[at, :] = tile
    halves = []
    for ref in (keep_ref, recv_ref):
        halves.append(jnp.concatenate(
            [
                ref[h, HALF : HALF + 1, 0:HEAD].astype(F32)
                + ref[h, HALF : HALF + 1, 128 : 128 + HEAD].astype(F32)
                for h in range(2)
            ],
            axis=1,
        ))
    row = lax.broadcasted_iota(jnp.int32, (2, 2 * HEAD), 0)
    gradient = jnp.where(row == core, halves[0], halves[1])
    master = master_ref[...]
    new_first = BETA_ONE * first_ref[...] + (1.0 - BETA_ONE) * gradient
    new_second = BETA_TWO * second_ref[...] + (1.0 - BETA_TWO) * gradient * gradient
    direction = (
        new_first
        / (1.0 - BETA_ONE**STEP)
        / (jnp.sqrt(new_second / (1.0 - BETA_TWO**STEP)) + ADAM_EPSILON)
    )
    nm_ref[...] = master - LEARN_RATE * (direction + WEIGHT_DECAY * master)
    nf_ref[...] = new_first
    ns_ref[...] = new_second


def exchange(value, axes):
    return lax.all_to_all(value, axes, split_axis=0, concat_axis=0, tiled=True)


def swap(value):
    return lax.ppermute(value, "core", [(0, 1), (1, 0)])


def copies(value, count):
    return jnp.broadcast_to(value[None], (count, *value.shape)).reshape(
        count * value.shape[0], *value.shape[1:]
    )


def body(normed, w_down, query, key, value_base, cotangent, master, first, second):
    core = lax.axis_index("core")
    pos = jnp.stack([lax.axis_index(a) for a in ("y", "zh", "x", "zl", "core")]).astype(jnp.int32)

    rows = lax.all_gather(master.astype(BF), "core", axis=0)
    rows = rows.reshape(2, 2, 2, HEAD).transpose(0, 2, 1, 3).reshape(4, 2, HEAD)
    rows = jnp.pad(rows, ((0, 0), (0, 0), (0, LANES - HEAD)))
    rows = jnp.broadcast_to(rows[None, :, None], (4, 4, 4, 2, LANES)).reshape(64, 2, LANES)
    w_up = exchange(rows, ("y", "zh", "x")).reshape(RANK, LANES)

    part, keep, send = call(
        pack_kernel,
        [((8, HALF, RANK), F32), ((2, HALF, 512), BF), ((2, HALF, 512), BF)],
        [SMEM] + [VMEM] * 6,
    )(pos, normed, w_down, query, cotangent, key, value_base)
    part = exchange(part, ("zl", "core"))
    recv = swap(send)
    (pieces,) = call(route_kernel, [((4, HALF, 640), BF)], [SMEM] + [VMEM] * 3)(
        pos, part, keep, recv
    )
    pieces = exchange(pieces, "zh").reshape(256, 640)
    q_tile = exchange(copies(pieces[:, 0:256], 4), "x")
    k_own = exchange(copies(pieces[:, 256:640], 4), "y")
    k_other = swap(k_own)

    stat, values = call(
        first_kernel, [((8, N_Q), F32), ((N_K, LANES), BF)], [SMEM] + [VMEM] * 4
    )(pos, q_tile, k_own, k_other, w_up)
    stats = exchange(jnp.broadcast_to(stat[None], (4, 8, N_Q)), "x")
    dq, dk_keep, dk_send, grad = call(
        second_kernel,
        [((N_Q, LANES), BF), ((1024, LANES), F32), ((1024, LANES), BF), ((RANK, LANES), F32)],
        [SMEM] + [VMEM] * 5,
        [pltpu.VMEM((N_K, LANES), F32)] * 2,
    )(pos, q_tile, k_own, k_other, values, stats)
    dq = exchange(dq.reshape(4, 256, LANES), "x")
    dk = (dk_keep + swap(dk_send).astype(F32)).astype(BF)
    dk = exchange(dk.reshape(4, 256, LANES), "y")
    grad = exchange(grad.reshape(32, 4, LANES), ("y", "x", "core"))
    (back,) = call(sums_kernel, [((4, HALF + 16, 256), BF)], [VMEM] * 3)(dq, dk, grad)
    back = exchange(back, "zh")
    keep = lax.dynamic_slice_in_dim(back, core * 2, 2, 0)
    recv = swap(lax.dynamic_slice_in_dim(back, (1 - core) * 2, 2, 0))
    return tuple(call(
        last_kernel,
        [((TOK, 2 * HEAD), BF)] * 2 + [((2, 2 * HEAD), F32)] * 3,
        [SMEM] + [VMEM] * 5,
    )(pos, keep, recv, master, first, second))


def solution(mesh):
    fine = Mesh(mesh.devices.reshape(4, 4, 4, 4, 2), ("y", "zh", "x", "zl", "core"))
    seq, section = ("y", "zh", "x"), ("zl", "core")
    split = P(seq, section)
    return jax.shard_map(
        body,
        mesh=fine,
        in_specs=(split, P(section, None)) + (split,) * 7,
        out_specs=(split,) * 5,
        check_vma=False,
    )
```

```python
import math

import jax
import jax.numpy as jnp
from jax import lax
from jax.experimental import pallas as pl
from jax.experimental.pallas import tpu as pltpu
from jax.sharding import Mesh, PartitionSpec as P

HEAD = 112
LANES = 128
RANK = 128
STEP = 2

BETA_ONE = 0.9
BETA_TWO = 0.95
LEARN_RATE = 0.01
WEIGHT_DECAY = 0.1
ADAM_EPSILON = 1e-08
MASK_VALUE = -1e30
LOW_MAX = -1e20
SCORE_SCALE = 1.0 / math.sqrt(HEAD)
INV_RANK = 1.0 / math.sqrt(RANK)

BF = jnp.bfloat16
F32 = jnp.float32

TOK = 128
HALF = 64
N_Q = 1024
N_K = 2048
Q_STEP = 256
VMEM_LIMIT = 56 * 1024 * 1024

VMEM = pl.BlockSpec(memory_space=pltpu.VMEM)
SMEM = pl.BlockSpec(memory_space=pltpu.SMEM)


def call(kernel, shapes, specs, scratch=()):
    return pl.pallas_call(
        kernel,
        out_shape=[jax.ShapeDtypeStruct(s, d) for s, d in shapes],
        in_specs=specs,
        out_specs=[VMEM] * len(shapes),
        scratch_shapes=list(scratch),
        compiler_params=pltpu.CompilerParams(vmem_limit_bytes=VMEM_LIMIT),
    )


def dot_nt(a, b):
    return lax.dot_general(a, b, (((1,), (1,)), ((), ())), preferred_element_type=F32)


def dot_tn(a, b):
    return lax.dot_general(a, b, (((0,), (0,)), ((), ())), preferred_element_type=F32)


def rank_of(order):
    return (
        ((order >> 4) & 3) * 32 + (order & 3) * 8 + ((order >> 2) & 3) * 2 + (order >> 6)
    )


def iotas(rows, cols):
    return (
        lax.broadcasted_iota(jnp.int32, (rows, cols), 0),
        lax.broadcasted_iota(jnp.int32, (rows, cols), 1),
    )


def one_hot(mask):
    return jnp.where(mask, 1.0, 0.0).astype(BF)


def split(value):
    high = value.astype(BF)
    return high, (value - high.astype(F32)).astype(BF)


def pack_kernel(pos, x_ref, wd_ref, q_ref, do_ref, k_ref, vb_ref, m_ref,
                part_ref, keep_ref, send_ref, full, w_pad):
    core = pos[4]
    part = dot_tn(x_ref[...], wd_ref[...])
    for s in range(8):
        h = s % 2
        part_ref[s] = part[h * HALF : (h + 1) * HALF]
    full[...] = jnp.zeros_like(full)
    for i, ref in enumerate((q_ref, do_ref, k_ref, vb_ref)):
        for h in range(2):
            tile = ref[h * HEAD : (h + 1) * HEAD, :].T
            full[h, :, i * LANES : i * LANES + HEAD] = tile
    w_pad[...] = jnp.zeros_like(w_pad)
    w_pad[0:2, 0 : 2 * HEAD] = m_ref[...]
    rows = w_pad[...].astype(BF)
    src, dst = iotas(8, LANES)
    for h in range(2):
        spread = sum(
            dot_tn(
                rows[:, h * HEAD + d * HALF : h * HEAD + (d + 1) * HALF],
                one_hot((src < 2) & (dst == HEAD + 2 * d + src)),
            )
            for d in range(2)
        ).astype(BF)
        for t in range(2):
            at = slice(t * HALF, (t + 1) * HALF)
            full[h, at, 384:512] = full[h, at, 384:512] + spread
    own = pl.ds(pl.multiple_of(core * HALF, HALF), HALF)
    other = pl.ds(pl.multiple_of((1 - core) * HALF, HALF), HALF)
    for h in range(2):
        keep_ref[h] = full[h, own, :]
        send_ref[h] = full[h, other, :]


def route_kernel(pos, part_ref, keep_ref, recv_ref, out_ref):
    core = pos[4]
    total = part_ref[0]
    for s in range(1, 8):
        total = total + part_ref[s]
    src, dst = iotas(RANK, RANK)
    order = one_hot(src == rank_of(dst))
    low = jnp.dot(total.astype(BF), order, preferred_element_type=F32).astype(BF)
    for j in range(4):
        out_ref[j, :, 512:640] = low
    for h in range(2):
        out_ref[core * 2 + h, :, 0:512] = keep_ref[h]
        out_ref[(1 - core) * 2 + h, :, 0:512] = recv_ref[h]


def mix_kernel(q_ref, k_ref, out_ref):
    lane = lax.broadcasted_iota(jnp.int32, (256, LANES), 1)
    here = (lane >= HEAD) & (lane < HEAD + 4)
    total = q_ref[:, 0:128].astype(F32)
    for y in range(4):
        tile = k_ref[y * 256 : (y + 1) * 256, 128:256].astype(F32)
        tile = jnp.where(here, tile, 0.0)
        total = total + (pltpu.roll(tile, 4 * y, 1) if y else tile)
    total = total.astype(BF)
    for i in range(4):
        out_ref[i, :, 0:128] = total
        out_ref[i, :, 128:256] = q_ref[:, 128:256]


def token_ids(pos):
    y, x, core = pos[0], pos[2], pos[4]
    n = lax.broadcasted_iota(jnp.int32, (1, N_Q), 1)
    q_tok = y * 2048 + ((n >> 6) & 3) * 512 + (n >> 8) * 128 + core * HALF + (n & 63)
    m = lax.broadcasted_iota(jnp.int32, (N_K, 1), 0)
    half = (m >> 10) ^ core
    k_tok = ((m >> 8) & 3) * 2048 + ((m >> 6) & 3) * 512 + x * 128 + half * HALF + (m & 63)
    return q_tok, k_tok


def up_rows(q_ref):
    src, dst = iotas(LANES, RANK)
    lane = src - HEAD
    halves = []
    for d in range(2):
        place = one_hot(
            (lane >= 0) & (((lane >> 1) & 1) == d) & (dst == (lane & 1) * 64 + (lane >> 2) * 16)
        )
        spread = jnp.dot(q_ref[:, 0:128], place, preferred_element_type=F32)
        total = spread[0:HALF]
        for b in range(1, 16):
            tile = spread[b * HALF : (b + 1) * HALF]
            total = total + pltpu.roll(tile, b, 1)
        halves.append(total)
    return jnp.concatenate(halves, axis=0).astype(BF)


def first_kernel(pos, q_ref, own_ref, other_ref, stat_ref, v_ref):
    w_up = up_rows(q_ref)
    for h, ref in enumerate((own_ref, other_ref)):
        add = dot_nt(ref[:, 256:384], w_up) * INV_RANK
        v_ref[h * 1024 : (h + 1) * 1024] = (ref[:, 128:256].astype(F32) + add).astype(BF)
    q_tok, k_tok = token_ids(pos)
    keys = jnp.concatenate([own_ref[:, 0:128], other_ref[:, 0:128]], axis=0)
    values = v_ref[...]
    for s in range(N_Q // Q_STEP):
        cols = slice(s * Q_STEP, (s + 1) * Q_STEP)
        scores = dot_nt(keys, q_ref[cols, 0:128]) * SCORE_SCALE
        scores = jnp.where(k_tok <= q_tok[:, cols], scores, MASK_VALUE)
        top = jnp.maximum(jnp.max(scores, axis=0, keepdims=True), LOW_MAX)
        weight = jnp.exp(scores - top)
        total = jnp.sum(weight, axis=0, keepdims=True)
        d_prob = dot_nt(values, q_ref[cols, 128:256])
        delta = jnp.sum(weight * d_prob, axis=0, keepdims=True)
        some = total > 0.0
        safe = jnp.where(some, total, 1.0)
        log_total = jnp.where(some, top + jnp.log(safe), MASK_VALUE)
        for i in range(4):
            stat_ref[i, s : s + 1, :] = log_total
            stat_ref[i, 4 + s : 5 + s, :] = delta / safe


def second_kernel(pos, q_ref, own_ref, other_ref, v_ref, stat_ref,
                  dq_ref, keep_ref, send_ref, gkeep_ref, dk_acc, dv_acc, grad_acc):
    core = pos[4]
    q_tok, k_tok = token_ids(pos)
    keys = jnp.concatenate([own_ref[:, 0:128], other_ref[:, 0:128]], axis=0)
    low = jnp.concatenate([own_ref[:, 256:384], other_ref[:, 256:384]], axis=0)
    values = v_ref[...]
    for s in range(N_Q // Q_STEP):
        cols = slice(s * Q_STEP, (s + 1) * Q_STEP)
        lse = [stat_ref[i, s : s + 1, :] for i in range(4)]
        top = jnp.maximum(jnp.maximum(lse[0], lse[1]), jnp.maximum(lse[2], lse[3]))
        share = [jnp.exp(l - top) for l in lse]
        total = share[0] + share[1] + share[2] + share[3]
        delta = sum(share[i] * stat_ref[i, 4 + s : 5 + s, :] for i in range(4)) / total
        log_total = top + jnp.log(total)
        queries, cotan = q_ref[cols, 0:128], q_ref[cols, 128:256]
        scores = dot_nt(keys, queries) * SCORE_SCALE
        scores = jnp.where(k_tok <= q_tok[:, cols], scores, MASK_VALUE)
        prob = jnp.exp(scores - log_total)
        d_prob = dot_nt(values, cotan)
        d_score = (prob * (d_prob - delta)).astype(BF)
        d_key = jnp.dot(d_score, queries, preferred_element_type=F32)
        d_val = jnp.dot(prob.astype(BF), cotan, preferred_element_type=F32)
        if s == 0:
            dk_acc[...] = d_key
            dv_acc[...] = d_val
        else:
            dk_acc[...] += d_key
            dv_acc[...] += d_val
        dq_ref[cols, :] = (dot_tn(d_score, keys) * SCORE_SCALE).astype(BF)
    keep_ref[...] = dk_acc[0:1024] * SCORE_SCALE
    send_ref[0:1024] = (dk_acc[1024:2048] * SCORE_SCALE).astype(BF)
    grad_acc[...] = dot_tn(low, dv_acc[...].astype(BF)) * INV_RANK
    gkeep_ref[...] = grad_acc[pl.ds(pl.multiple_of(core * 64, 64), 64), :]
    high, rest = split(grad_acc[pl.ds(pl.multiple_of((1 - core) * 64, 64), 64), :])
    send_ref[1024:1088] = high
    send_ref[1088:1152] = rest


def core_sum_kernel(keep_ref, gkeep_ref, recv_ref, out_ref):
    for y in range(4):
        at = slice(y * 256, (y + 1) * 256)
        out_ref[y, 0:256] = (keep_ref[at] + recv_ref[at].astype(F32)).astype(BF)
        rows = slice(y * 16, (y + 1) * 16)
        grad = (
            gkeep_ref[rows]
            + recv_ref[1024 + y * 16 : 1040 + y * 16].astype(F32)
            + recv_ref[1088 + y * 16 : 1104 + y * 16].astype(F32)
        )
        out_ref[y, 256:272], out_ref[y, 272:288] = split(grad)


def total_of(ref, rows):
    total = ref[0, rows].astype(F32)
    for i in range(1, 4):
        total = total + ref[i, rows].astype(F32)
    return total


def y_sum_kernel(dk_ref, dq_ref, dk_out, out_ref):
    dk_out[...] = total_of(dk_ref, slice(0, 256)).astype(BF)
    grad = total_of(dk_ref, slice(256, 272)) + total_of(dk_ref, slice(272, 288))
    high, rest = split(grad)
    for i in range(4):
        out_ref[i, 0:256] = dq_ref[i * 256 : (i + 1) * 256]
        out_ref[i, 256:272] = high
        out_ref[i, 272:288] = rest


def x_sum_kernel(dq_ref, dk_ref, out_ref):
    dq = total_of(dq_ref, slice(0, 256)).astype(BF)
    grad = total_of(dq_ref, slice(256, 272)) + total_of(dq_ref, slice(272, 288))
    high, rest = split(grad)
    for z in range(4):
        rows = slice(z * HALF, (z + 1) * HALF)
        out_ref[z, 0:HALF, 0:128] = dq[rows]
        out_ref[z, 0:HALF, 128:256] = dk_ref[rows]
        out_ref[z, HALF : HALF + 16, 0:128] = high
        out_ref[z, HALF : HALF + 16, 128:256] = rest


def last_kernel(pos, keep_ref, recv_ref, master_ref, first_ref, second_ref,
                qg_ref, kg_ref, nm_ref, nf_ref, ns_ref, tile_ref):
    z_hi, x, core = pos[1], pos[2], pos[4]
    for half, ref in ((core, keep_ref), (1 - core, recv_ref)):
        at = pl.ds(pl.multiple_of(half * HALF, HALF), HALF)
        for h in range(2):
            tile_ref[h, at, :] = ref[h, 0:HALF, :]
    for out, lane in ((qg_ref, 0), (kg_ref, 128)):
        for h in range(2):
            out[h * HEAD : (h + 1) * HEAD, :] = tile_ref[h, :, lane : lane + LANES].T[0:HEAD]
    row16 = lax.broadcasted_iota(jnp.int32, (16, LANES), 0)
    mine = row16 == x * 4 + z_hi
    halves = []
    for ref in (keep_ref, recv_ref):
        parts = []
        for h in range(2):
            rows = ref[h, HALF : HALF + 16, :].astype(F32)
            rows = jnp.where(mine, rows[:, 0:128] + rows[:, 128:256], 0.0)
            parts.append(jnp.sum(rows, axis=0, keepdims=True)[:, 0:HEAD])
        halves.append(jnp.concatenate(parts, axis=1))
    row = lax.broadcasted_iota(jnp.int32, (2, 2 * HEAD), 0)
    gradient = jnp.where(row == core, halves[0], halves[1])
    master = master_ref[...]
    new_first = BETA_ONE * first_ref[...] + (1.0 - BETA_ONE) * gradient
    new_second = BETA_TWO * second_ref[...] + (1.0 - BETA_TWO) * gradient * gradient
    direction = (
        new_first
        / (1.0 - BETA_ONE**STEP)
        / (jnp.sqrt(new_second / (1.0 - BETA_TWO**STEP)) + ADAM_EPSILON)
    )
    nm_ref[...] = master - LEARN_RATE * (direction + WEIGHT_DECAY * master)
    nf_ref[...] = new_first
    ns_ref[...] = new_second


def exchange(value, axes):
    return lax.all_to_all(value, axes, split_axis=0, concat_axis=0, tiled=True)


def swap(value):
    return lax.ppermute(value, "core", [(0, 1), (1, 0)])


def copies(value, count):
    return jnp.broadcast_to(value[None], (count, *value.shape)).reshape(
        count * value.shape[0], *value.shape[1:]
    )


def body(normed, w_down, query, key, value_base, cotangent, master, first, second):
    core = lax.axis_index("core")
    pos = jnp.stack([lax.axis_index(a) for a in ("y", "zh", "x", "zl", "core")]).astype(jnp.int32)

    part, keep, send = call(
        pack_kernel,
        [((8, HALF, RANK), F32), ((2, HALF, 512), BF), ((2, HALF, 512), BF)],
        [SMEM] + [VMEM] * 7,
        [pltpu.VMEM((2, TOK, 512), BF), pltpu.VMEM((8, 256), F32)],
    )(pos, normed.T, w_down, query.T, cotangent.T, key.T, value_base.T, master)
    part = exchange(part, ("zl", "core"))
    recv = swap(send)
    (pieces,) = call(route_kernel, [((4, HALF, 640), BF)], [SMEM] + [VMEM] * 3)(
        pos, part, keep, recv
    )
    pieces = exchange(pieces, "zh").reshape(256, 640)
    k_own = exchange(copies(pieces[:, 256:640], 4), "y")
    k_other = swap(k_own)
    (q_tile,) = call(mix_kernel, [((4, 256, 256), BF)], [VMEM] * 2)(pieces[:, 0:256], k_own)
    q_tile = exchange(q_tile, "x").reshape(N_Q, 256)

    stat, values = call(
        first_kernel, [((4, 8, Q_STEP), F32), ((N_K, LANES), BF)], [SMEM] + [VMEM] * 3
    )(pos, q_tile, k_own, k_other)
    stats = exchange(stat, "x")
    dq, dk_keep, dk_send, g_keep = call(
        second_kernel,
        [((N_Q, LANES), BF), ((1024, LANES), F32), ((1152, LANES), BF), ((64, LANES), F32)],
        [SMEM] + [VMEM] * 5,
        [pltpu.VMEM((N_K, LANES), F32)] * 2 + [pltpu.VMEM((RANK, LANES), F32)],
    )(pos, q_tile, k_own, k_other, values, stats)
    (dk,) = call(core_sum_kernel, [((4, 288, LANES), BF)], [VMEM] * 3)(
        dk_keep, g_keep, swap(dk_send)
    )
    dk, dq = call(y_sum_kernel, [((256, LANES), BF), ((4, 288, LANES), BF)], [VMEM] * 2)(
        exchange(dk, "y"), dq
    )
    (back,) = call(x_sum_kernel, [((4, HALF + 16, 256), BF)], [VMEM] * 2)(exchange(dq, "x"), dk)
    back = exchange(back, "zh")
    keep = lax.dynamic_slice_in_dim(back, core * 2, 2, 0)
    recv = swap(lax.dynamic_slice_in_dim(back, (1 - core) * 2, 2, 0))
    q_grad, k_grad, new_master, new_first, new_second = call(
        last_kernel,
        [((2 * HEAD, TOK), BF)] * 2 + [((2, 2 * HEAD), F32)] * 3,
        [SMEM] + [VMEM] * 5,
        [pltpu.VMEM((2, TOK, 2 * LANES), BF)],
    )(pos, keep, recv, master, first, second)
    return q_grad.T, k_grad.T, new_master, new_first, new_second


def solution(mesh):
    fine = Mesh(mesh.devices.reshape(4, 4, 4, 4, 2), ("y", "zh", "x", "zl", "core"))
    seq, section = ("y", "zh", "x"), ("zl", "core")
    split = P(seq, section)
    return jax.shard_map(
        body,
        mesh=fine,
        in_specs=(split, P(section, None)) + (split,) * 7,
        out_specs=(split,) * 5,
        check_vma=False,
    )
```

```python
import math

import jax
import jax.numpy as jnp
from jax import lax
from jax.experimental import pallas as pl
from jax.experimental.pallas import tpu as pltpu
from jax.sharding import Mesh, PartitionSpec as P

HEAD = 112
LANES = 128
RANK = 128
STEP = 2

BETA_ONE = 0.9
BETA_TWO = 0.95
LEARN_RATE = 0.01
WEIGHT_DECAY = 0.1
ADAM_EPSILON = 1e-08
MASK_VALUE = -1e30
LOW_MAX = -1e20
SCORE_SCALE = 1.0 / math.sqrt(HEAD)
INV_RANK = 1.0 / math.sqrt(RANK)

BF = jnp.bfloat16
F32 = jnp.float32

TOK = 128
HALF = 64
N_Q = 1024
N_K = 2048
Q_STEP = 256
K_STEP = 512
LOG2_E = math.log2(math.e)

VMEM = pl.BlockSpec(memory_space=pltpu.VMEM)


def call(kernel, shapes, args, outer=(), scratch=(), limit=8, pinned=True):
    return pl.pallas_call(
        kernel,
        out_shape=[(pltpu.VMEM if pinned else jax.ShapeDtypeStruct)(s, d) for s, d in shapes],
        in_specs=[VMEM] * (len(args) + len(outer)),
        out_specs=[VMEM] * len(shapes),
        scratch_shapes=list(scratch),
        compiler_params=pltpu.CompilerParams(vmem_limit_bytes=limit * 1024 * 1024),
    )(*[pltpu.with_memory_space_constraint(a, pltpu.VMEM) for a in args], *outer)


def dot_nt(a, b):
    return lax.dot_general(a, b, (((1,), (1,)), ((), ())), preferred_element_type=F32)


def dot_tn(a, b):
    return lax.dot_general(a, b, (((0,), (0,)), ((), ())), preferred_element_type=F32)


def rank_of(order):
    return (
        ((order >> 3) & 3) * 32 + (order & 3) * 8 + (order >> 5) * 2 + ((order >> 2) & 1)
    )


def iotas(rows, cols):
    return (
        lax.broadcasted_iota(jnp.int32, (rows, cols), 0),
        lax.broadcasted_iota(jnp.int32, (rows, cols), 1),
    )


def one_hot(mask):
    return jnp.where(mask, 1.0, 0.0).astype(BF)


def split(value):
    high = value.astype(BF)
    return high, (value - high.astype(F32)).astype(BF)


def pack_kernel(x_ref, wd_ref, q_ref, do_ref, k_ref, vb_ref, m_ref,
                part_ref, keep_ref, send_ref, full, w_pad):
    core = lax.axis_index("core")
    part = dot_tn(x_ref[...], wd_ref[...]).astype(BF)
    for s in range(8):
        h = s % 2
        part_ref[s] = part[h * HALF : (h + 1) * HALF]
    full[...] = jnp.zeros_like(full)
    for i, ref in enumerate((q_ref, do_ref, k_ref, vb_ref)):
        for h in range(2):
            tile = ref[h * HEAD : (h + 1) * HEAD, :].T
            full[h, :, i * LANES : i * LANES + HEAD] = tile
    w_pad[...] = jnp.zeros_like(w_pad)
    w_pad[0:2, 0 : 2 * HEAD] = m_ref[...]
    rows = w_pad[...].astype(BF)
    src, dst = iotas(8, LANES)
    for h in range(2):
        spread = sum(
            dot_tn(
                rows[:, h * HEAD + d * HALF : h * HEAD + (d + 1) * HALF],
                one_hot((src < 2) & (dst == HEAD + 2 * d + src)),
            )
            for d in range(2)
        ).astype(BF)
        for t in range(2):
            at = slice(t * HALF, (t + 1) * HALF)
            full[h, at, 384:512] = full[h, at, 384:512] + spread
    own = pl.ds(pl.multiple_of(core * HALF, HALF), HALF)
    other = pl.ds(pl.multiple_of((1 - core) * HALF, HALF), HALF)
    for h in range(2):
        keep_ref[h] = full[h, own, :]
        send_ref[h] = full[h, other, :]


def route_kernel(part_ref, keep_ref, recv_ref, out_ref):
    core = lax.axis_index("core")
    total = part_ref[0].astype(F32)
    for s in range(1, 8):
        total = total + part_ref[s].astype(F32)
    src, dst = iotas(RANK, RANK)
    order = one_hot(src == rank_of(dst))
    low = jnp.dot(total.astype(BF), order, preferred_element_type=F32).astype(BF)
    for j in range(4):
        out_ref[j, :, 512:640] = low
    for h in range(2):
        out_ref[core * 2 + h, :, 0:512] = keep_ref[h]
        out_ref[(1 - core) * 2 + h, :, 0:512] = recv_ref[h]


def mix_kernel(piece_ref, k_ref, out_ref):
    lane = lax.broadcasted_iota(jnp.int32, (256, LANES), 1)
    here = (lane >= HEAD) & (lane < HEAD + 4)
    total = piece_ref[:, 0:128].astype(F32)
    for y in range(4):
        tile = k_ref[y * 256 : (y + 1) * 256, 128:256].astype(F32)
        tile = jnp.where(here, tile, 0.0)
        total = total + (pltpu.roll(tile, 4 * y, 1) if y else tile)
    total = total.astype(BF)
    for i in range(4):
        out_ref[i, :, 0:128] = total
        out_ref[i, :, 128:256] = piece_ref[:, 128:256]


def diagonal_mask(half):
    x, core = lax.axis_index("x"), lax.axis_index("core")
    n = lax.broadcasted_iota(jnp.int32, (1, N_Q), 1)
    q_tok = ((n >> 6) & 3) * 512 + (n >> 8) * 128 + core * HALF + (n & 63)
    m = lax.broadcasted_iota(jnp.int32, (256, 1), 0)
    k_tok = (m >> 6) * 512 + x * 128 + (core ^ half) * HALF + (m & 63)
    return q_tok, k_tok


def up_rows(q_ref):
    src, dst = iotas(LANES, RANK)
    lane = src - HEAD
    halves = []
    for d in range(2):
        place = one_hot(
            (lane >= 0) & (((lane >> 1) & 1) == d) & (dst == (lane & 1) * 4 + (lane >> 2) * 8)
        )
        spread = jnp.dot(q_ref[:, 0:128], place, preferred_element_type=F32)
        total = spread[0:HALF]
        for b in range(1, 16):
            tile = spread[b * HALF : (b + 1) * HALF]
            total = total + pltpu.roll(tile, (b >> 2) * 32 + (b & 3), 1)
        halves.append(total)
    return jnp.concatenate(halves, axis=0).astype(BF)


def first_kernel(q_ref, own_ref, other_ref, stat_ref, top_ref, w_ref, d_ref, v_ref):
    w_up = up_rows(q_ref)
    for h, ref in enumerate((own_ref, other_ref)):
        add = dot_nt(ref[:, 256:384], w_up) * INV_RANK
        v_ref[h * 1024 : (h + 1) * 1024] = (ref[:, 128:256].astype(F32) + add).astype(BF)
    y = lax.axis_index("y")
    keys = jnp.concatenate([own_ref[:, 0:128], other_ref[:, 0:128]], axis=0)
    values = v_ref[...]
    for s in range(N_Q // Q_STEP):
        cols = slice(s * Q_STEP, (s + 1) * Q_STEP)
        w_ref[:, cols] = dot_nt(keys, q_ref[cols, 0:128]) * (SCORE_SCALE * LOG2_E)
        for half in range(2):
            q_tok, k_tok = diagonal_mask(half)
            rows = pl.ds(pl.multiple_of(half * 1024 + y * 256, 256), 256)
            w_ref[rows, cols] = jnp.where(k_tok <= q_tok[:, cols], w_ref[rows, cols], MASK_VALUE)
            for block in range(1, 4):
                @pl.when(block > y)
                def _():
                    later = slice(half * 1024 + block * 256, half * 1024 + block * 256 + 256)
                    w_ref[later, cols] = jnp.full((256, Q_STEP), MASK_VALUE, F32)
        d_ref[:, cols] = dot_nt(values, q_ref[cols, 128:256])
        scores = w_ref[:, cols]
        top = jnp.maximum(jnp.max(scores, axis=0, keepdims=True), LOW_MAX)
        weight = jnp.exp2(scores - top)
        w_ref[:, cols] = weight
        total = jnp.sum(weight, axis=0, keepdims=True)
        delta = jnp.sum(weight * d_ref[:, cols], axis=0, keepdims=True)
        some = total > 0.0
        safe = jnp.where(some, total, 1.0)
        log_total = jnp.where(some, top + jnp.log2(safe), MASK_VALUE)
        top_ref[0:1, cols] = top
        for i in range(4):
            stat_ref[i, 0:1, cols] = log_total
            stat_ref[i, 1:2, cols] = delta / safe


def second_kernel(q_ref, own_ref, other_ref, w_ref, d_ref, top_ref, stat_ref,
                  dq_ref, keep_ref, send_ref, dv_ref, dq_acc):
    lse = [stat_ref[i, 0:1, :] for i in range(4)]
    top = jnp.maximum(jnp.maximum(lse[0], lse[1]), jnp.maximum(lse[2], lse[3]))
    share = [jnp.exp2(l - top) for l in lse]
    total = share[0] + share[1] + share[2] + share[3]
    delta = sum(share[i] * stat_ref[i, 1:2, :] for i in range(4)) / total
    factor = jnp.exp2(top_ref[0:1, :] - (top + jnp.log2(total)))
    queries, cotan = q_ref[:, 0:128], q_ref[:, 128:256]
    for s in range(N_K // K_STEP):
        rows = slice(s * K_STEP, (s + 1) * K_STEP)
        ref, out = (own_ref, keep_ref) if s < 2 else (other_ref, send_ref)
        part = slice((s % 2) * K_STEP, (s % 2 + 1) * K_STEP)
        prob = w_ref[rows] * factor
        d_score = (prob * (d_ref[rows] - delta)).astype(BF)
        dv_ref[rows] = jnp.dot(prob.astype(BF), cotan, preferred_element_type=F32).astype(BF)
        d_key = jnp.dot(d_score, queries, preferred_element_type=F32) * SCORE_SCALE
        out[part] = d_key.astype(out.dtype)
        d_query = dot_tn(ref[part, 0:128], d_score)
        if s == 0:
            dq_acc[...] = d_query
        else:
            dq_acc[...] += d_query
    d_query = (dq_acc[...] * SCORE_SCALE).T.astype(BF)
    low = jnp.concatenate([own_ref[:, 256:384], other_ref[:, 256:384]], axis=0)
    high, rest = split(dot_tn(low, dv_ref[...]) * INV_RANK)
    for i in range(4):
        dq_ref[i, 0:256] = d_query[i * 256 : (i + 1) * 256]
        dq_ref[i, 256:288] = high[i * 32 : (i + 1) * 32]
        dq_ref[i, 288:320] = rest[i * 32 : (i + 1) * 32]


def total_of(ref, rows):
    total = ref[0, rows].astype(F32)
    for i in range(1, 4):
        total = total + ref[i, rows].astype(F32)
    return total


def pair(value):
    high, rest = split(value)
    return jnp.concatenate([high.astype(F32), rest.astype(F32)], axis=0).astype(BF)


def x_sum_kernel(dq_ref, keep_ref, recv_ref, dq_out, out_ref):
    dq_out[...] = total_of(dq_ref, slice(0, 256)).astype(BF)
    grad = total_of(dq_ref, slice(256, 288)) + total_of(dq_ref, slice(288, 320))
    for y in range(4):
        at = slice(y * 256, (y + 1) * 256)
        out_ref[y, 0:256] = (keep_ref[at] + recv_ref[at].astype(F32)).astype(BF)
        out_ref[y, 256:272] = pair(grad[y * 8 : (y + 1) * 8])


def y_sum_kernel(dk_ref, dq_ref, out_ref):
    dk = total_of(dk_ref, slice(0, 256)).astype(BF)
    grad = total_of(dk_ref, slice(256, 272))
    grad = pair(grad[0:8] + grad[8:16])
    for z in range(4):
        rows = slice(z * HALF, (z + 1) * HALF)
        out_ref[z, 0:HALF, 0:128] = dq_ref[rows]
        out_ref[z, 0:HALF, 128:256] = dk[rows]
        out_ref[z, HALF : HALF + 16, 0:128] = grad
        out_ref[z, HALF : HALF + 16, 128:256] = jnp.zeros((16, 128), BF)


def last_kernel(back_ref, master_ref, first_ref, second_ref,
                qg_ref, kg_ref, nm_ref, nf_ref, ns_ref, tile_ref):
    z_hi, core = lax.axis_index("zh"), lax.axis_index("core")
    for half in range(2):
        for h in range(2):
            tile_ref[h, half * HALF : (half + 1) * HALF] = back_ref[half, core * 2 + h, 0:HALF, :]
    for out, lane in ((qg_ref, 0), (kg_ref, 128)):
        for h in range(2):
            out[h * HEAD : (h + 1) * HEAD, :] = tile_ref[h, :, lane : lane + LANES].T[0:HEAD]
    row8 = lax.broadcasted_iota(jnp.int32, (8, LANES), 0)
    columns = []
    for h in range(2):
        rows = (
            back_ref[0, core * 2 + h, HALF : HALF + 16, 0:128].astype(F32)
            + back_ref[1, core * 2 + h, HALF : HALF + 16, 0:128].astype(F32)
        )
        rows = rows[0:8] + rows[8:16]
        columns.append(jnp.concatenate(
            [
                jnp.sum(jnp.where(row8 == e * 4 + z_hi, rows, 0.0), axis=0, keepdims=True)
                for e in range(2)
            ],
            axis=0,
        )[:, 0:HEAD])
    gradient = jnp.concatenate(columns, axis=1)
    master = master_ref[...]
    new_first = BETA_ONE * first_ref[...] + (1.0 - BETA_ONE) * gradient
    new_second = BETA_TWO * second_ref[...] + (1.0 - BETA_TWO) * gradient * gradient
    direction = (
        new_first
        / (1.0 - BETA_ONE**STEP)
        / (jnp.sqrt(new_second / (1.0 - BETA_TWO**STEP)) + ADAM_EPSILON)
    )
    nm_ref[...] = master - LEARN_RATE * (direction + WEIGHT_DECAY * master)
    nf_ref[...] = new_first
    ns_ref[...] = new_second


def exchange(value, axes):
    return lax.all_to_all(value, axes, split_axis=0, concat_axis=0, tiled=True)


def swap(value):
    return lax.ppermute(value, "core", [(0, 1), (1, 0)])


def copies(value, count):
    return jnp.broadcast_to(value[None], (count, *value.shape)).reshape(
        count * value.shape[0], *value.shape[1:]
    )


def body(normed, w_down, query, key, value_base, cotangent, master, first, second):
    part, keep, send = call(
        pack_kernel,
        [((8, HALF, RANK), BF), ((2, HALF, 512), BF), ((2, HALF, 512), BF)],
        (),
        (normed.T, w_down, query.T, cotangent.T, key.T, value_base.T, master),
        [pltpu.VMEM((2, TOK, 512), BF), pltpu.VMEM((8, 256), F32)],
        limit=56,
    )
    part = exchange(part, ("zl", "core"))
    recv = swap(send)
    (pieces,) = call(route_kernel, [((4, HALF, 640), BF)], (part, keep, recv))
    pieces = exchange(pieces, "zh").reshape(256, 640)
    k_own = exchange(copies(pieces[:, 256:640], 4), "y")
    k_other = swap(k_own)
    (q_tile,) = call(mix_kernel, [((4, 256, 256), BF)], (pieces, k_own))
    q_tile = exchange(q_tile, "x").reshape(N_Q, 256)

    stat, top, weight, d_prob = call(
        first_kernel,
        [((4, 2, N_Q), F32), ((1, N_Q), F32), ((N_K, N_Q), F32), ((N_K, N_Q), F32)],
        (q_tile, k_own, k_other),
        scratch=[pltpu.VMEM((N_K, LANES), BF)],
        limit=16,
    )
    stats = exchange(stat, "x")
    dq, dk_keep, dk_send = call(
        second_kernel,
        [((4, 320, LANES), BF), ((1024, LANES), F32), ((1024, LANES), BF)],
        (q_tile, k_own, k_other, weight, d_prob, top, stats),
        scratch=[pltpu.VMEM((N_K, LANES), BF), pltpu.VMEM((LANES, N_Q), F32)],
        limit=16,
    )
    dk_recv = swap(dk_send)
    dq, dk = call(
        x_sum_kernel,
        [((256, LANES), BF), ((4, 272, LANES), BF)],
        (exchange(dq, "x"), dk_keep, dk_recv),
    )
    (back,) = call(y_sum_kernel, [((4, HALF + 16, 256), BF)], (exchange(dk, "y"), dq))
    back = exchange(back, "zh")
    back = lax.all_gather(back, "core", axis=0)
    q_grad, k_grad, new_master, new_first, new_second = call(
        last_kernel,
        [((2 * HEAD, TOK), BF)] * 2 + [((2, 2 * HEAD), F32)] * 3,
        (back,),
        (master, first, second),
        [pltpu.VMEM((2, TOK, 2 * LANES), BF)],
        pinned=False,
    )
    return q_grad.T, k_grad.T, new_master, new_first, new_second


def solution(mesh):
    fine = Mesh(mesh.devices.reshape(4, 4, 4, 4, 2), ("y", "zh", "x", "zl", "core"))
    seq, section = ("y", "zh", "x"), ("zl", "core")
    split = P(seq, section)
    return jax.shard_map(
        body,
        mesh=fine,
        in_specs=(split, P(section, None)) + (split,) * 7,
        out_specs=(split,) * 5,
        check_vma=False,
    )
```

```python
import math

import jax
import jax.numpy as jnp
from jax import lax
from jax.experimental import pallas as pl
from jax.experimental.pallas import tpu as pltpu
from jax.sharding import Mesh, PartitionSpec as P

HEAD = 112
LANES = 128
RANK = 128
STEP = 2

BETA_ONE = 0.9
BETA_TWO = 0.95
LEARN_RATE = 0.01
WEIGHT_DECAY = 0.1
ADAM_EPSILON = 1e-08
MASK_VALUE = -1e30
LOW_MAX = -1e20
SCORE_SCALE = 1.0 / math.sqrt(HEAD)
INV_RANK = 1.0 / math.sqrt(RANK)

BF = jnp.bfloat16
F32 = jnp.float32

TOK = 128
HALF = 64
N_Q = 1024
N_K = 2048
K_BLOCK = 256
K_STEP = 512
LOG2_E = math.log2(math.e)

VMEM = pl.BlockSpec(memory_space=pltpu.VMEM)


def call(kernel, shapes, args, outer=(), scratch=(), limit=8, pinned=True):
    return pl.pallas_call(
        kernel,
        out_shape=[(pltpu.VMEM if pinned else jax.ShapeDtypeStruct)(s, d) for s, d in shapes],
        in_specs=[VMEM] * (len(args) + len(outer)),
        out_specs=[VMEM] * len(shapes),
        scratch_shapes=list(scratch),
        compiler_params=pltpu.CompilerParams(vmem_limit_bytes=limit * 1024 * 1024),
    )(*[pltpu.with_memory_space_constraint(a, pltpu.VMEM) for a in args], *outer)


def dot_nt(a, b):
    return lax.dot_general(a, b, (((1,), (1,)), ((), ())), preferred_element_type=F32)


def dot_tn(a, b):
    return lax.dot_general(a, b, (((0,), (0,)), ((), ())), preferred_element_type=F32)


def rank_of(order):
    return (
        ((order >> 3) & 3) * 32 + (order & 3) * 8 + (order >> 5) * 2 + ((order >> 2) & 1)
    )


def iotas(rows, cols):
    return (
        lax.broadcasted_iota(jnp.int32, (rows, cols), 0),
        lax.broadcasted_iota(jnp.int32, (rows, cols), 1),
    )


def one_hot(mask):
    return jnp.where(mask, 1.0, 0.0).astype(BF)


def split(value):
    high = value.astype(BF)
    return high, (value - high.astype(F32)).astype(BF)


def low_kernel(x_ref, wd_ref, part_ref):
    part = dot_tn(x_ref[...], wd_ref[...]).astype(BF)
    for s in range(8):
        h = s % 2
        part_ref[s] = part[h * HALF : (h + 1) * HALF]


def pack_kernel(q_ref, do_ref, k_ref, vb_ref, m_ref, keep_ref, send_ref, full, w_pad):
    core = lax.axis_index("core")
    full[...] = jnp.zeros_like(full)
    for i, ref in enumerate((q_ref, do_ref, k_ref, vb_ref)):
        for h in range(2):
            tile = ref[h * HEAD : (h + 1) * HEAD, :].T
            full[h, :, i * LANES : i * LANES + HEAD] = tile
    w_pad[...] = jnp.zeros_like(w_pad)
    w_pad[0:2, 0 : 2 * HEAD] = m_ref[...]
    rows = w_pad[...].astype(BF)
    src, dst = iotas(8, LANES)
    for h in range(2):
        spread = sum(
            dot_tn(
                rows[:, h * HEAD + d * HALF : h * HEAD + (d + 1) * HALF],
                one_hot((src < 2) & (dst == HEAD + 2 * d + src)),
            )
            for d in range(2)
        ).astype(BF)
        for t in range(2):
            at = slice(t * HALF, (t + 1) * HALF)
            full[h, at, 384:512] = full[h, at, 384:512] + spread
    own = pl.ds(pl.multiple_of(core * HALF, HALF), HALF)
    other = pl.ds(pl.multiple_of((1 - core) * HALF, HALF), HALF)
    for h in range(2):
        keep_ref[h] = full[h, own, :]
        send_ref[h] = full[h, other, :]


def route_kernel(part_ref, keep_ref, recv_ref, out_ref):
    core = lax.axis_index("core")
    total = part_ref[0].astype(F32)
    for s in range(1, 8):
        total = total + part_ref[s].astype(F32)
    src, dst = iotas(RANK, RANK)
    order = one_hot(src == rank_of(dst))
    low = jnp.dot(total.astype(BF), order, preferred_element_type=F32).astype(BF)
    for j in range(4):
        out_ref[j, :, 512:640] = low
    for h in range(2):
        out_ref[core * 2 + h, :, 0:512] = keep_ref[h]
        out_ref[(1 - core) * 2 + h, :, 0:512] = recv_ref[h]


def mix_kernel(piece_ref, k_ref, out_ref):
    lane = lax.broadcasted_iota(jnp.int32, (256, LANES), 1)
    here = (lane >= HEAD) & (lane < HEAD + 4)
    total = piece_ref[:, 0:128].astype(F32)
    for y in range(4):
        tile = k_ref[y * 256 : (y + 1) * 256, 128:256].astype(F32)
        tile = jnp.where(here, tile, 0.0)
        total = total + (pltpu.roll(tile, 4 * y, 1) if y else tile)
    total = total.astype(BF)
    for i in range(4):
        out_ref[i, :, 0:128] = total
        out_ref[i, :, 128:256] = piece_ref[:, 128:256]


def token_ids():
    y, x, core = lax.axis_index("y"), lax.axis_index("x"), lax.axis_index("core")
    n = lax.broadcasted_iota(jnp.int32, (1, N_Q), 1)
    q_tok = y * 2048 + ((n >> 6) & 3) * 512 + (n >> 8) * 128 + core * HALF + (n & 63)
    m = lax.broadcasted_iota(jnp.int32, (N_K, 1), 0)
    k_y, half = (m >> 10) * 2 + ((m >> 8) & 1), (m >> 9) & 1
    k_tok = k_y * 2048 + ((m >> 6) & 3) * 512 + x * 128 + half * HALF + (m & 63)
    return q_tok, k_tok


def fold(value, op):
    return op(value.reshape(value.shape[0] // 8, 8, value.shape[1]), axis=0)


def up_rows(q_ref):
    src, dst = iotas(LANES, RANK)
    lane = src - HEAD
    halves = []
    for d in range(2):
        place = one_hot(
            (lane >= 0) & (((lane >> 1) & 1) == d) & (dst == (lane & 1) * 4 + (lane >> 2) * 8)
        )
        spread = jnp.dot(q_ref[:, 0:128], place, preferred_element_type=F32)
        total = spread[0:HALF]
        for b in range(1, 16):
            tile = spread[b * HALF : (b + 1) * HALF]
            total = total + pltpu.roll(tile, (b >> 2) * 32 + (b & 3), 1)
        halves.append(total)
    return jnp.concatenate(halves, axis=0).astype(BF)


def first_kernel(q_ref, low_ref, high_ref, stat_ref, top_ref, w_ref, d_ref, v_ref):
    w_up = up_rows(q_ref)
    for h, ref in enumerate((low_ref, high_ref)):
        add = dot_nt(ref[:, 256:384], w_up) * INV_RANK
        v_ref[h * 1024 : (h + 1) * 1024] = (ref[:, 128:256].astype(F32) + add).astype(BF)
    q_tok, k_tok = token_ids()
    queries, cotan = q_ref[:, 0:128], q_ref[:, 128:256]
    highest = None
    for start in range(0, N_K, K_BLOCK):
        ref = low_ref if start < 1024 else high_ref
        part = slice(start % 1024, start % 1024 + K_BLOCK)
        rows = slice(start, start + K_BLOCK)
        scores = jnp.where(k_tok[rows] <= q_tok, dot_nt(ref[part, 0:128], queries), MASK_VALUE)
        w_ref[rows] = scores
        block = fold(scores, jnp.max)
        highest = block if highest is None else jnp.maximum(highest, block)
    scale = SCORE_SCALE * LOG2_E
    top = jnp.maximum(jnp.max(highest, axis=0, keepdims=True) * scale, LOW_MAX)
    total = delta = jnp.zeros((8, N_Q), F32)
    for start in range(0, N_K, K_BLOCK):
        rows = slice(start, start + K_BLOCK)
        weight = jnp.exp2(w_ref[rows] * scale - top)
        w_ref[rows] = weight
        d_prob = dot_nt(v_ref[rows], cotan)
        d_ref[rows] = d_prob
        total = total + fold(weight, jnp.sum)
        delta = delta + fold(weight * d_prob, jnp.sum)
    total = jnp.sum(total, axis=0, keepdims=True)
    delta = jnp.sum(delta, axis=0, keepdims=True)
    some = total > 0.0
    safe = jnp.where(some, total, 1.0)
    top_ref[...] = top
    for i in range(4):
        stat_ref[i, 0:1] = jnp.where(some, top + jnp.log2(safe), MASK_VALUE)
        stat_ref[i, 1:2] = delta / safe


def second_kernel(q_ref, low_ref, high_ref, w_ref, d_ref, top_ref, stat_ref,
                  dq_ref, dk_ref, dv_ref, dq_acc):
    lse = [stat_ref[i, 0:1, :] for i in range(4)]
    top = jnp.maximum(jnp.maximum(lse[0], lse[1]), jnp.maximum(lse[2], lse[3]))
    share = [jnp.exp2(l - top) for l in lse]
    total = share[0] + share[1] + share[2] + share[3]
    delta = sum(share[i] * stat_ref[i, 1:2, :] for i in range(4)) / total
    factor = jnp.exp2(top_ref[0:1, :] - (top + jnp.log2(total)))
    queries, cotan = q_ref[:, 0:128], q_ref[:, 128:256]
    for s in range(N_K // K_STEP):
        rows = slice(s * K_STEP, (s + 1) * K_STEP)
        ref = low_ref if s < 2 else high_ref
        part = slice((s % 2) * K_STEP, (s % 2 + 1) * K_STEP)
        prob = w_ref[rows] * factor
        d_score = (prob * (d_ref[rows] - delta)).astype(BF)
        dv_ref[rows] = jnp.dot(prob.astype(BF), cotan, preferred_element_type=F32).astype(BF)
        dk_ref[rows] = jnp.dot(d_score, queries, preferred_element_type=F32)
        d_query = dot_tn(ref[part, 0:128], d_score)
        if s == 0:
            dq_acc[...] = d_query
        else:
            dq_acc[...] += d_query
    d_query = (dq_acc[...] * SCORE_SCALE).T.astype(BF)
    low = jnp.concatenate([low_ref[:, 256:384], high_ref[:, 256:384]], axis=0)
    high, rest = split(dot_tn(low, dv_ref[...]) * INV_RANK)
    for i in range(4):
        dq_ref[i, 0:256] = d_query[i * 256 : (i + 1) * 256]
        dq_ref[i, 256:288] = high[i * 32 : (i + 1) * 32]
        dq_ref[i, 288:320] = rest[i * 32 : (i + 1) * 32]


def scale_kernel(dk_ref, keep_ref, send_ref):
    core = lax.axis_index("core")
    for g in range(2):
        own = pl.ds(pl.multiple_of(g * 1024 + core * 512, 512), 512)
        other = pl.ds(pl.multiple_of(g * 1024 + (1 - core) * 512, 512), 512)
        keep_ref[g * 512 : (g + 1) * 512] = dk_ref[own] * SCORE_SCALE
        send_ref[g * 512 : (g + 1) * 512] = (dk_ref[other] * SCORE_SCALE).astype(BF)


def total_of(ref, rows):
    total = ref[0, rows].astype(F32)
    for i in range(1, 4):
        total = total + ref[i, rows].astype(F32)
    return total


def pair(value):
    high, rest = split(value)
    return jnp.concatenate([high.astype(F32), rest.astype(F32)], axis=0).astype(BF)


def x_sum_kernel(dq_ref, keep_ref, recv_ref, dq_out, out_ref):
    other = 1 - lax.axis_index("core")
    dq_out[...] = total_of(dq_ref, slice(0, 256)).astype(BF)
    grad = total_of(dq_ref, slice(256, 288)) + total_of(dq_ref, slice(288, 320))
    for y in range(4):
        at = slice(y * 256, (y + 1) * 256)
        out_ref[y, 0:256] = (keep_ref[at] + recv_ref[other, at].astype(F32)).astype(BF)
        out_ref[y, 256:272] = pair(grad[y * 8 : (y + 1) * 8])


def y_sum_kernel(dk_ref, dq_ref, out_ref):
    dk = total_of(dk_ref, slice(0, 256)).astype(BF)
    grad = total_of(dk_ref, slice(256, 272))
    grad = pair(grad[0:8] + grad[8:16])
    for z in range(4):
        rows = slice(z * HALF, (z + 1) * HALF)
        out_ref[z, 0:HALF, 0:128] = dq_ref[rows]
        out_ref[z, 0:HALF, 128:256] = dk[rows]
        out_ref[z, HALF : HALF + 16, 0:128] = grad
        out_ref[z, HALF : HALF + 16, 128:256] = jnp.zeros((16, 128), BF)


def last_kernel(back_ref, master_ref, first_ref, second_ref,
                qg_ref, kg_ref, nm_ref, nf_ref, ns_ref, tile_ref):
    z_hi, core = lax.axis_index("zh"), lax.axis_index("core")
    for half in range(2):
        for h in range(2):
            tile_ref[h, half * HALF : (half + 1) * HALF] = back_ref[half, core * 2 + h, 0:HALF, :]
    for out, lane in ((qg_ref, 0), (kg_ref, 128)):
        for h in range(2):
            out[h * HEAD : (h + 1) * HEAD, :] = tile_ref[h, :, lane : lane + LANES].T[0:HEAD]
    row8 = lax.broadcasted_iota(jnp.int32, (8, LANES), 0)
    columns = []
    for h in range(2):
        rows = (
            back_ref[0, core * 2 + h, HALF : HALF + 16, 0:128].astype(F32)
            + back_ref[1, core * 2 + h, HALF : HALF + 16, 0:128].astype(F32)
        )
        rows = rows[0:8] + rows[8:16]
        columns.append(jnp.concatenate(
            [
                jnp.sum(jnp.where(row8 == e * 4 + z_hi, rows, 0.0), axis=0, keepdims=True)
                for e in range(2)
            ],
            axis=0,
        )[:, 0:HEAD])
    gradient = jnp.concatenate(columns, axis=1)
    master = master_ref[...]
    new_first = BETA_ONE * first_ref[...] + (1.0 - BETA_ONE) * gradient
    new_second = BETA_TWO * second_ref[...] + (1.0 - BETA_TWO) * gradient * gradient
    direction = (
        new_first
        / (1.0 - BETA_ONE**STEP)
        / (jnp.sqrt(new_second / (1.0 - BETA_TWO**STEP)) + ADAM_EPSILON)
    )
    nm_ref[...] = master - LEARN_RATE * (direction + WEIGHT_DECAY * master)
    nf_ref[...] = new_first
    ns_ref[...] = new_second


def exchange(value, axes):
    return lax.all_to_all(value, axes, split_axis=0, concat_axis=0, tiled=True)


def swap(value):
    return lax.ppermute(value, "core", [(0, 1), (1, 0)])


def copies(value, count):
    return jnp.broadcast_to(value[None], (count, *value.shape)).reshape(
        count * value.shape[0], *value.shape[1:]
    )


def both_cores(value):
    return lax.all_gather(value, "core", axis=0)


def body(normed, w_down, query, key, value_base, cotangent, master, first, second):
    (part,) = call(low_kernel, [((8, HALF, RANK), BF)], (), (normed.T, w_down), limit=56)
    keep, send = call(
        pack_kernel,
        [((2, HALF, 512), BF), ((2, HALF, 512), BF)],
        (),
        (query.T, cotangent.T, key.T, value_base.T, master),
        [pltpu.VMEM((2, TOK, 512), BF), pltpu.VMEM((8, 256), F32)],
        limit=56,
    )
    part = exchange(part, ("zl", "core"))
    recv = swap(send)
    (pieces,) = call(route_kernel, [((4, HALF, 640), BF)], (part, keep, recv))
    pieces = exchange(pieces, "zh").reshape(256, 640)
    k_own = exchange(copies(pieces[:, 256:640], 4), "y")
    (q_tile,) = call(mix_kernel, [((4, 256, 256), BF)], (pieces, k_own))
    k_low = both_cores(k_own[0:512]).reshape(1024, 384)
    k_high = both_cores(k_own[512:1024]).reshape(1024, 384)
    q_tile = exchange(q_tile, "x").reshape(N_Q, 256)

    stat, top, weight, d_prob = call(
        first_kernel,
        [((4, 2, N_Q), F32), ((1, N_Q), F32), ((N_K, N_Q), F32), ((N_K, N_Q), F32)],
        (q_tile, k_low, k_high),
        scratch=[pltpu.VMEM((N_K, LANES), BF)],
        limit=24,
    )
    stats = exchange(stat, "x")
    dq, dk = call(
        second_kernel,
        [((4, 320, LANES), BF), ((N_K, LANES), F32)],
        (q_tile, k_low, k_high, weight, d_prob, top, stats),
        scratch=[pltpu.VMEM((N_K, LANES), BF), pltpu.VMEM((LANES, N_Q), F32)],
        limit=16,
    )
    dk_keep, dk_send = call(
        scale_kernel, [((1024, LANES), F32), ((1024, LANES), BF)], (dk,)
    )
    dk_recv = both_cores(dk_send)
    dq, dk = call(
        x_sum_kernel,
        [((256, LANES), BF), ((4, 272, LANES), BF)],
        (exchange(dq, "x"), dk_keep, dk_recv),
    )
    (back,) = call(y_sum_kernel, [((4, HALF + 16, 256), BF)], (exchange(dk, "y"), dq))
    back = exchange(back, "zh")
    back = both_cores(back)
    q_grad, k_grad, new_master, new_first, new_second = call(
        last_kernel,
        [((2 * HEAD, TOK), BF)] * 2 + [((2, 2 * HEAD), F32)] * 3,
        (back,),
        (master, first, second),
        [pltpu.VMEM((2, TOK, 2 * LANES), BF)],
        pinned=False,
    )
    return q_grad.T, k_grad.T, new_master, new_first, new_second


def solution(mesh):
    fine = Mesh(mesh.devices.reshape(4, 4, 4, 4, 2), ("y", "zh", "x", "zl", "core"))
    seq, section = ("y", "zh", "x"), ("zl", "core")
    split = P(seq, section)
    return jax.shard_map(
        body,
        mesh=fine,
        in_specs=(split, P(section, None)) + (split,) * 7,
        out_specs=(split,) * 5,
        check_vma=False,
    )
```

```python
import math

import jax
import jax.numpy as jnp
from jax import lax
from jax.experimental import pallas as pl
from jax.experimental.pallas import tpu as pltpu
from jax.sharding import Mesh, PartitionSpec as P

HEAD = 112
LANES = 128
RANK = 128
STEP = 2

BETA_ONE = 0.9
BETA_TWO = 0.95
LEARN_RATE = 0.01
WEIGHT_DECAY = 0.1
ADAM_EPSILON = 1e-08
MASK_VALUE = -1e30
LOW_MAX = -1e20
SCORE_SCALE = 1.0 / math.sqrt(HEAD)
INV_RANK = 1.0 / math.sqrt(RANK)

BF = jnp.bfloat16
F32 = jnp.float32

TOK = 128
HALF = 64
N_Q = 1024
N_K = 2048
K_BLOCK = 256
K_STEP = 512
LOG2_E = math.log2(math.e)

VMEM = pl.BlockSpec(memory_space=pltpu.VMEM)


def call(kernel, shapes, args, outer=(), scratch=(), limit=8, pinned=True):
    return pl.pallas_call(
        kernel,
        out_shape=[(pltpu.VMEM if pinned else jax.ShapeDtypeStruct)(s, d) for s, d in shapes],
        in_specs=[VMEM] * (len(args) + len(outer)),
        out_specs=[VMEM] * len(shapes),
        scratch_shapes=list(scratch),
        compiler_params=pltpu.CompilerParams(vmem_limit_bytes=limit * 1024 * 1024),
    )(*[pltpu.with_memory_space_constraint(a, pltpu.VMEM) for a in args], *outer)


def dot_nt(a, b):
    return lax.dot_general(a, b, (((1,), (1,)), ((), ())), preferred_element_type=F32)


def dot_tn(a, b):
    return lax.dot_general(a, b, (((0,), (0,)), ((), ())), preferred_element_type=F32)


def rank_of(order):
    return (
        ((order >> 3) & 3) * 32 + (order & 3) * 8 + (order >> 5) * 2 + ((order >> 2) & 1)
    )


def iotas(rows, cols):
    return (
        lax.broadcasted_iota(jnp.int32, (rows, cols), 0),
        lax.broadcasted_iota(jnp.int32, (rows, cols), 1),
    )


def one_hot(mask):
    return jnp.where(mask, 1.0, 0.0).astype(BF)


def split(value):
    high = value.astype(BF)
    return high, (value - high.astype(F32)).astype(BF)


def low_kernel(x_ref, wd_ref, part_ref):
    part_ref[...] = dot_tn(x_ref[...], wd_ref[...])


def half_kernel(part_ref, out_ref):
    rows = pl.ds(pl.multiple_of(lax.axis_index("core") * HALF, HALF), HALF)
    total = part_ref[0, rows] + part_ref[1, rows]
    for s in range(4):
        out_ref[s] = total


def pack_kernel(q_ref, do_ref, k_ref, vb_ref, m_ref, keep_ref, send_ref, full, w_pad):
    core = lax.axis_index("core")
    full[...] = jnp.zeros_like(full)
    for i, ref in enumerate((q_ref, do_ref, k_ref, vb_ref)):
        for h in range(2):
            tile = ref[h * HEAD : (h + 1) * HEAD, :].T
            full[h, :, i * LANES : i * LANES + HEAD] = tile
    w_pad[...] = jnp.zeros_like(w_pad)
    w_pad[0:2, 0 : 2 * HEAD] = m_ref[...]
    rows = w_pad[...].astype(BF)
    src, dst = iotas(8, LANES)
    for h in range(2):
        spread = sum(
            dot_tn(
                rows[:, h * HEAD + d * HALF : h * HEAD + (d + 1) * HALF],
                one_hot((src < 2) & (dst == HEAD + 2 * d + src)),
            )
            for d in range(2)
        ).astype(BF)
        for t in range(2):
            at = slice(t * HALF, (t + 1) * HALF)
            full[h, at, 384:512] = full[h, at, 384:512] + spread
    own = pl.ds(pl.multiple_of(core * HALF, HALF), HALF)
    other = pl.ds(pl.multiple_of((1 - core) * HALF, HALF), HALF)
    for h in range(2):
        keep_ref[h] = full[h, own, :]
        send_ref[h] = full[h, other, :]


def route_kernel(part_ref, keep_ref, recv_ref, out_ref):
    core = lax.axis_index("core")
    total = part_ref[0] + part_ref[1] + part_ref[2] + part_ref[3]
    src, dst = iotas(RANK, RANK)
    order = one_hot(src == rank_of(dst))
    low = jnp.dot(total.astype(BF), order, preferred_element_type=F32).astype(BF)
    for j in range(4):
        out_ref[j, :, 512:640] = low
    for h in range(2):
        out_ref[core * 2 + h, :, 0:512] = keep_ref[h]
        out_ref[(1 - core) * 2 + h, :, 0:512] = recv_ref[h]


def mix_kernel(piece_ref, k_ref, out_ref):
    lane = lax.broadcasted_iota(jnp.int32, (256, LANES), 1)
    here = (lane >= HEAD) & (lane < HEAD + 4)
    total = piece_ref[:, 0:128].astype(F32)
    for y in range(4):
        tile = k_ref[y * 256 : (y + 1) * 256, 128:256].astype(F32)
        tile = jnp.where(here, tile, 0.0)
        total = total + (pltpu.roll(tile, 4 * y, 1) if y else tile)
    total = total.astype(BF)
    for i in range(4):
        out_ref[i, :, 0:128] = total
        out_ref[i, :, 128:256] = piece_ref[:, 128:256]


def token_ids():
    y, x, core = lax.axis_index("y"), lax.axis_index("x"), lax.axis_index("core")
    n = lax.broadcasted_iota(jnp.int32, (1, N_Q), 1)
    q_tok = y * 2048 + ((n >> 6) & 3) * 512 + (n >> 8) * 128 + core * HALF + (n & 63)
    m = lax.broadcasted_iota(jnp.int32, (N_K, 1), 0)
    k_y, half = (m >> 10) * 2 + ((m >> 8) & 1), (m >> 9) & 1
    k_tok = k_y * 2048 + ((m >> 6) & 3) * 512 + x * 128 + half * HALF + (m & 63)
    return q_tok, k_tok


def fold(value, op):
    return op(value.reshape(value.shape[0] // 8, 8, value.shape[1]), axis=0)


def up_rows(q_ref):
    src, dst = iotas(LANES, RANK)
    lane = src - HEAD
    halves = []
    for d in range(2):
        place = one_hot(
            (lane >= 0) & (((lane >> 1) & 1) == d) & (dst == (lane & 1) * 4 + (lane >> 2) * 8)
        )
        spread = jnp.dot(q_ref[:, 0:128], place, preferred_element_type=F32)
        total = spread[0:HALF]
        for b in range(1, 16):
            tile = spread[b * HALF : (b + 1) * HALF]
            total = total + pltpu.roll(tile, (b >> 2) * 32 + (b & 3), 1)
        halves.append(total)
    return jnp.concatenate(halves, axis=0).astype(BF)


def first_kernel(q_ref, low_ref, high_ref, stat_ref, top_ref, w_ref, d_ref, v_ref):
    w_up = up_rows(q_ref)
    for h, ref in enumerate((low_ref, high_ref)):
        add = dot_nt(ref[:, 256:384], w_up) * INV_RANK
        v_ref[h * 1024 : (h + 1) * 1024] = (ref[:, 128:256].astype(F32) + add).astype(BF)
    q_tok, k_tok = token_ids()
    queries, cotan = q_ref[:, 0:128], q_ref[:, 128:256]
    highest = None
    for start in range(0, N_K, K_BLOCK):
        ref = low_ref if start < 1024 else high_ref
        part = slice(start % 1024, start % 1024 + K_BLOCK)
        rows = slice(start, start + K_BLOCK)
        scores = jnp.where(k_tok[rows] <= q_tok, dot_nt(ref[part, 0:128], queries), MASK_VALUE)
        w_ref[rows] = scores
        block = fold(scores, jnp.max)
        highest = block if highest is None else jnp.maximum(highest, block)
    scale = SCORE_SCALE * LOG2_E
    top = jnp.maximum(jnp.max(highest, axis=0, keepdims=True) * scale, LOW_MAX)
    total = delta = jnp.zeros((8, N_Q), F32)
    for start in range(0, N_K, K_BLOCK):
        rows = slice(start, start + K_BLOCK)
        weight = jnp.exp2(w_ref[rows] * scale - top)
        w_ref[rows] = weight
        d_prob = dot_nt(v_ref[rows], cotan)
        d_ref[rows] = d_prob
        total = total + fold(weight, jnp.sum)
        delta = delta + fold(weight * d_prob, jnp.sum)
    total = jnp.sum(total, axis=0, keepdims=True)
    delta = jnp.sum(delta, axis=0, keepdims=True)
    some = total > 0.0
    safe = jnp.where(some, total, 1.0)
    top_ref[...] = top
    for i in range(4):
        stat_ref[i, 0:1] = jnp.where(some, top + jnp.log2(safe), MASK_VALUE)
        stat_ref[i, 1:2] = delta / safe


def second_kernel(q_ref, low_ref, high_ref, w_ref, d_ref, top_ref, stat_ref,
                  dq_ref, dk_ref, dv_ref, dq_acc):
    lse = [stat_ref[i, 0:1, :] for i in range(4)]
    top = jnp.maximum(jnp.maximum(lse[0], lse[1]), jnp.maximum(lse[2], lse[3]))
    share = [jnp.exp2(l - top) for l in lse]
    total = share[0] + share[1] + share[2] + share[3]
    delta = sum(share[i] * stat_ref[i, 1:2, :] for i in range(4)) / total
    factor = jnp.exp2(top_ref[0:1, :] - (top + jnp.log2(total)))
    queries, cotan = q_ref[:, 0:128], q_ref[:, 128:256]
    for s in range(N_K // K_STEP):
        rows = slice(s * K_STEP, (s + 1) * K_STEP)
        ref = low_ref if s < 2 else high_ref
        part = slice((s % 2) * K_STEP, (s % 2 + 1) * K_STEP)
        prob = w_ref[rows] * factor
        d_score = (prob * (d_ref[rows] - delta)).astype(BF)
        dv_ref[rows] = jnp.dot(prob.astype(BF), cotan, preferred_element_type=F32).astype(BF)
        dk_ref[rows] = jnp.dot(d_score, queries, preferred_element_type=F32)
        d_query = dot_tn(ref[part, 0:128], d_score)
        if s == 0:
            dq_acc[...] = d_query
        else:
            dq_acc[...] += d_query
    d_query = (dq_acc[...] * SCORE_SCALE).T.astype(BF)
    low = jnp.concatenate([low_ref[:, 256:384], high_ref[:, 256:384]], axis=0)
    high, rest = split(dot_tn(low, dv_ref[...]) * INV_RANK)
    for i in range(4):
        dq_ref[i, 0:256] = d_query[i * 256 : (i + 1) * 256]
        dq_ref[i, 256:288] = high[i * 32 : (i + 1) * 32]
        dq_ref[i, 288:320] = rest[i * 32 : (i + 1) * 32]


def scale_kernel(dk_ref, keep_ref, send_ref):
    core = lax.axis_index("core")
    for g in range(2):
        own = pl.ds(pl.multiple_of(g * 1024 + core * 512, 512), 512)
        other = pl.ds(pl.multiple_of(g * 1024 + (1 - core) * 512, 512), 512)
        keep_ref[g * 512 : (g + 1) * 512] = dk_ref[own] * SCORE_SCALE
        send_ref[g * 512 : (g + 1) * 512] = (dk_ref[other] * SCORE_SCALE).astype(BF)


def total_of(ref, rows):
    total = ref[0, rows].astype(F32)
    for i in range(1, 4):
        total = total + ref[i, rows].astype(F32)
    return total


def pair(value):
    high, rest = split(value)
    return jnp.concatenate([high.astype(F32), rest.astype(F32)], axis=0).astype(BF)


def x_sum_kernel(dq_ref, keep_ref, recv_ref, dq_out, out_ref):
    other = 1 - lax.axis_index("core")
    dq_out[...] = total_of(dq_ref, slice(0, 256)).astype(BF)
    grad = total_of(dq_ref, slice(256, 288)) + total_of(dq_ref, slice(288, 320))
    for y in range(4):
        at = slice(y * 256, (y + 1) * 256)
        out_ref[y, 0:256] = (keep_ref[at] + recv_ref[other, at].astype(F32)).astype(BF)
        out_ref[y, 256:272] = pair(grad[y * 8 : (y + 1) * 8])


def y_sum_kernel(dk_ref, dq_ref, out_ref):
    dk = total_of(dk_ref, slice(0, 256)).astype(BF)
    grad = total_of(dk_ref, slice(256, 272))
    grad = pair(grad[0:8] + grad[8:16])
    for z in range(4):
        rows = slice(z * HALF, (z + 1) * HALF)
        out_ref[z, 0:HALF, 0:128] = dq_ref[rows]
        out_ref[z, 0:HALF, 128:256] = dk[rows]
        out_ref[z, HALF : HALF + 16, 0:128] = grad
        out_ref[z, HALF : HALF + 16, 128:256] = jnp.zeros((16, 128), BF)


def last_kernel(back_ref, master_ref, first_ref, second_ref,
                qg_ref, kg_ref, nm_ref, nf_ref, ns_ref, tile_ref):
    z_hi, core = lax.axis_index("zh"), lax.axis_index("core")
    for half in range(2):
        for h in range(2):
            tile_ref[h, half * HALF : (half + 1) * HALF] = back_ref[half, core * 2 + h, 0:HALF, :]
    for out, lane in ((qg_ref, 0), (kg_ref, 128)):
        for h in range(2):
            out[h * HEAD : (h + 1) * HEAD, :] = tile_ref[h, :, lane : lane + LANES].T[0:HEAD]
    row8 = lax.broadcasted_iota(jnp.int32, (8, LANES), 0)
    columns = []
    for h in range(2):
        rows = (
            back_ref[0, core * 2 + h, HALF : HALF + 16, 0:128].astype(F32)
            + back_ref[1, core * 2 + h, HALF : HALF + 16, 0:128].astype(F32)
        )
        rows = rows[0:8] + rows[8:16]
        columns.append(jnp.concatenate(
            [
                jnp.sum(jnp.where(row8 == e * 4 + z_hi, rows, 0.0), axis=0, keepdims=True)
                for e in range(2)
            ],
            axis=0,
        )[:, 0:HEAD])
    gradient = jnp.concatenate(columns, axis=1)
    master = master_ref[...]
    new_first = BETA_ONE * first_ref[...] + (1.0 - BETA_ONE) * gradient
    new_second = BETA_TWO * second_ref[...] + (1.0 - BETA_TWO) * gradient * gradient
    direction = (
        new_first
        / (1.0 - BETA_ONE**STEP)
        / (jnp.sqrt(new_second / (1.0 - BETA_TWO**STEP)) + ADAM_EPSILON)
    )
    nm_ref[...] = master - LEARN_RATE * (direction + WEIGHT_DECAY * master)
    nf_ref[...] = new_first
    ns_ref[...] = new_second


def exchange(value, axes):
    return lax.all_to_all(value, axes, split_axis=0, concat_axis=0, tiled=True)


def swap(value):
    return lax.ppermute(value, "core", [(0, 1), (1, 0)])


def copies(value, count):
    return jnp.broadcast_to(value[None], (count, *value.shape)).reshape(
        count * value.shape[0], *value.shape[1:]
    )


def both_cores(value):
    return lax.all_gather(value, "core", axis=0)


def body(normed, w_down, query, key, value_base, cotangent, master, first, second):
    (part,) = call(low_kernel, [((TOK, RANK), F32)], (), (normed.T, w_down), limit=56)
    (part,) = call(half_kernel, [((4, HALF, RANK), F32)], (both_cores(part),))
    keep, send = call(
        pack_kernel,
        [((2, HALF, 512), BF), ((2, HALF, 512), BF)],
        (),
        (query.T, cotangent.T, key.T, value_base.T, master),
        [pltpu.VMEM((2, TOK, 512), BF), pltpu.VMEM((8, 256), F32)],
        limit=56,
    )
    part = exchange(part, "zl")
    recv = swap(send)
    (pieces,) = call(route_kernel, [((4, HALF, 640), BF)], (part, keep, recv))
    pieces = exchange(pieces, "zh").reshape(256, 640)
    k_own = exchange(copies(pieces[:, 256:640], 4), "y")
    (q_tile,) = call(mix_kernel, [((4, 256, 256), BF)], (pieces, k_own))
    k_low = both_cores(k_own[0:512]).reshape(1024, 384)
    k_high = both_cores(k_own[512:1024]).reshape(1024, 384)
    q_tile = exchange(q_tile, "x").reshape(N_Q, 256)

    stat, top, weight, d_prob = call(
        first_kernel,
        [((4, 2, N_Q), F32), ((1, N_Q), F32), ((N_K, N_Q), F32), ((N_K, N_Q), F32)],
        (q_tile, k_low, k_high),
        scratch=[pltpu.VMEM((N_K, LANES), BF)],
        limit=24,
    )
    stats = exchange(stat, "x")
    dq, dk = call(
        second_kernel,
        [((4, 320, LANES), BF), ((N_K, LANES), F32)],
        (q_tile, k_low, k_high, weight, d_prob, top, stats),
        scratch=[pltpu.VMEM((N_K, LANES), BF), pltpu.VMEM((LANES, N_Q), F32)],
        limit=16,
    )
    dk_keep, dk_send = call(
        scale_kernel, [((1024, LANES), F32), ((1024, LANES), BF)], (dk,)
    )
    dk_recv = both_cores(dk_send)
    dq, dk = call(
        x_sum_kernel,
        [((256, LANES), BF), ((4, 272, LANES), BF)],
        (exchange(dq, "x"), dk_keep, dk_recv),
    )
    (back,) = call(y_sum_kernel, [((4, HALF + 16, 256), BF)], (exchange(dk, "y"), dq))
    back = exchange(back, "zh")
    back = both_cores(back)
    q_grad, k_grad, new_master, new_first, new_second = call(
        last_kernel,
        [((2 * HEAD, TOK), BF)] * 2 + [((2, 2 * HEAD), F32)] * 3,
        (back,),
        (master, first, second),
        [pltpu.VMEM((2, TOK, 2 * LANES), BF)],
        pinned=False,
    )
    return q_grad.T, k_grad.T, new_master, new_first, new_second


def solution(mesh):
    fine = Mesh(mesh.devices.reshape(4, 4, 4, 4, 2), ("y", "zh", "x", "zl", "core"))
    seq, section = ("y", "zh", "x"), ("zl", "core")
    split = P(seq, section)
    return jax.shard_map(
        body,
        mesh=fine,
        in_specs=(split, P(section, None)) + (split,) * 7,
        out_specs=(split,) * 5,
        check_vma=False,
    )
```

```python
import math

import jax
import jax.numpy as jnp
from jax import lax
from jax.experimental import pallas as pl
from jax.experimental.pallas import tpu as pltpu
from jax.sharding import Mesh, PartitionSpec as P

HEAD = 112
LANES = 128
RANK = 128
STEP = 2

BETA_ONE = 0.9
BETA_TWO = 0.95
LEARN_RATE = 0.01
WEIGHT_DECAY = 0.1
ADAM_EPSILON = 1e-08
MASK_VALUE = -1e30
LOW_MAX = -1e20
SCORE_SCALE = 1.0 / math.sqrt(HEAD)
INV_RANK = 1.0 / math.sqrt(RANK)

BF = jnp.bfloat16
F32 = jnp.float32

TOK = 128
HALF = 64
N_Q = 1024
N_K = 2048
K_BLOCK = 256
K_STEP = 512
LOG2_E = math.log2(math.e)

VMEM = pl.BlockSpec(memory_space=pltpu.VMEM)


def call(kernel, shapes, args, outer=(), scratch=(), limit=8, pinned=True):
    return pl.pallas_call(
        kernel,
        out_shape=[(pltpu.VMEM if pinned else jax.ShapeDtypeStruct)(s, d) for s, d in shapes],
        in_specs=[VMEM] * (len(args) + len(outer)),
        out_specs=[VMEM] * len(shapes),
        scratch_shapes=list(scratch),
        compiler_params=pltpu.CompilerParams(vmem_limit_bytes=limit * 1024 * 1024),
    )(*[pltpu.with_memory_space_constraint(a, pltpu.VMEM) for a in args], *outer)


def dot_nt(a, b):
    return lax.dot_general(a, b, (((1,), (1,)), ((), ())), preferred_element_type=F32)


def dot_tn(a, b):
    return lax.dot_general(a, b, (((0,), (0,)), ((), ())), preferred_element_type=F32)


def rank_of(order):
    return (
        ((order >> 3) & 3) * 32 + (order & 3) * 8 + (order >> 5) * 2 + ((order >> 2) & 1)
    )


def iotas(rows, cols):
    return (
        lax.broadcasted_iota(jnp.int32, (rows, cols), 0),
        lax.broadcasted_iota(jnp.int32, (rows, cols), 1),
    )


def one_hot(mask):
    return jnp.where(mask, 1.0, 0.0).astype(BF)


def split(value):
    high = value.astype(BF)
    return high, (value - high.astype(F32)).astype(BF)


def low_kernel(x_ref, wd_ref, part_ref):
    part_ref[...] = dot_tn(x_ref[...], wd_ref[...])


def half_kernel(part_ref, out_ref):
    rows = pl.ds(pl.multiple_of(lax.axis_index("core") * HALF, HALF), HALF)
    total = part_ref[0, rows] + part_ref[1, rows]
    for s in range(4):
        out_ref[s] = total


def pack_kernel(q_ref, do_ref, k_ref, vb_ref, m_ref, keep_ref, send_ref, full, w_pad):
    core = lax.axis_index("core")
    full[...] = jnp.zeros_like(full)
    for i, ref in enumerate((q_ref, do_ref, k_ref, vb_ref)):
        for h in range(2):
            tile = ref[h * HEAD : (h + 1) * HEAD, :].T
            full[h, :, i * LANES : i * LANES + HEAD] = tile
    w_pad[...] = jnp.zeros_like(w_pad)
    w_pad[0:2, 0 : 2 * HEAD] = m_ref[...]
    rows = w_pad[...].astype(BF)
    src, dst = iotas(16, LANES)
    for h in range(2):
        spread = sum(
            dot_tn(
                rows[:, h * HEAD + d * HALF : h * HEAD + (d + 1) * HALF],
                one_hot((src < 2) & (dst == HEAD + 2 * d + src)),
            )
            for d in range(2)
        ).astype(BF)
        for t in range(2):
            at = slice(t * HALF, (t + 1) * HALF)
            full[h, at, 384:512] = full[h, at, 384:512] + spread
    own = pl.ds(pl.multiple_of(core * HALF, HALF), HALF)
    other = pl.ds(pl.multiple_of((1 - core) * HALF, HALF), HALF)
    for h in range(2):
        keep_ref[h] = full[h, own, :]
        send_ref[h] = full[h, other, :]


def route_kernel(part_ref, keep_ref, recv_ref, out_ref):
    core = lax.axis_index("core")
    total = part_ref[0] + part_ref[1] + part_ref[2] + part_ref[3]
    src, dst = iotas(RANK, RANK)
    order = one_hot(src == rank_of(dst))
    low = jnp.dot(total.astype(BF), order, preferred_element_type=F32).astype(BF)
    for j in range(4):
        out_ref[j, :, 512:640] = low
    for h in range(2):
        out_ref[core * 2 + h, :, 0:512] = keep_ref[h]
        out_ref[(1 - core) * 2 + h, :, 0:512] = recv_ref[h]


def mix_kernel(piece_ref, k_ref, out_ref):
    lane = lax.broadcasted_iota(jnp.int32, (256, LANES), 1)
    here = (lane >= HEAD) & (lane < HEAD + 4)
    total = piece_ref[:, 0:128].astype(F32)
    for y in range(4):
        tile = k_ref[y * 256 : (y + 1) * 256, 128:256].astype(F32)
        tile = jnp.where(here, tile, 0.0)
        total = total + (pltpu.roll(tile, 4 * y, 1) if y else tile)
    total = total.astype(BF)
    for i in range(4):
        out_ref[i, :, 0:128] = total
        out_ref[i, :, 128:256] = piece_ref[:, 128:256]


def token_ids():
    y, x, core = lax.axis_index("y"), lax.axis_index("x"), lax.axis_index("core")
    n = lax.broadcasted_iota(jnp.int32, (1, N_Q), 1)
    q_tok = y * 2048 + ((n >> 6) & 3) * 512 + (n >> 8) * 128 + core * HALF + (n & 63)
    m = lax.broadcasted_iota(jnp.int32, (N_K, 1), 0)
    k_y, half = (m >> 10) * 2 + ((m >> 8) & 1), (m >> 9) & 1
    k_tok = k_y * 2048 + ((m >> 6) & 3) * 512 + x * 128 + half * HALF + (m & 63)
    return q_tok, k_tok


def fold(value, op):
    return op(value.reshape(value.shape[0] // 8, 8, value.shape[1]), axis=0)


def up_rows(q_ref):
    src, dst = iotas(LANES, RANK)
    lane = src - HEAD
    halves = []
    for d in range(2):
        place = one_hot(
            (lane >= 0) & (((lane >> 1) & 1) == d) & (dst == (lane & 1) * 4 + (lane >> 2) * 8)
        )
        spread = jnp.dot(q_ref[:, 0:128], place, preferred_element_type=F32)
        total = spread[0:HALF]
        for b in range(1, 16):
            tile = spread[b * HALF : (b + 1) * HALF]
            total = total + pltpu.roll(tile, (b >> 2) * 32 + (b & 3), 1)
        halves.append(total)
    return jnp.concatenate(halves, axis=0).astype(BF)


def first_kernel(q_ref, low_ref, high_ref, stat_ref, top_ref, w_ref, d_ref, v_ref):
    w_up = up_rows(q_ref)
    for h, ref in enumerate((low_ref, high_ref)):
        add = dot_nt(ref[:, 256:384], w_up) * INV_RANK
        v_ref[h * 1024 : (h + 1) * 1024] = (ref[:, 128:256].astype(F32) + add).astype(BF)
    q_tok, k_tok = token_ids()
    queries, cotan = q_ref[:, 0:128], q_ref[:, 128:256]
    highest = None
    for start in range(0, N_K, K_BLOCK):
        ref = low_ref if start < 1024 else high_ref
        part = slice(start % 1024, start % 1024 + K_BLOCK)
        rows = slice(start, start + K_BLOCK)
        scores = jnp.where(k_tok[rows] <= q_tok, dot_nt(ref[part, 0:128], queries), MASK_VALUE)
        w_ref[rows] = scores
        block = fold(scores, jnp.max)
        highest = block if highest is None else jnp.maximum(highest, block)
    scale = SCORE_SCALE * LOG2_E
    top = jnp.maximum(jnp.max(highest, axis=0, keepdims=True) * scale, LOW_MAX)
    total = delta = jnp.zeros((8, N_Q), F32)
    for start in range(0, N_K, K_BLOCK):
        rows = slice(start, start + K_BLOCK)
        weight = jnp.exp2(w_ref[rows] * scale - top)
        w_ref[rows] = weight
        d_prob = dot_nt(v_ref[rows], cotan)
        d_ref[rows] = d_prob
        total = total + fold(weight, jnp.sum)
        delta = delta + fold(weight * d_prob, jnp.sum)
    total = jnp.sum(total, axis=0, keepdims=True)
    delta = jnp.sum(delta, axis=0, keepdims=True)
    some = total > 0.0
    safe = jnp.where(some, total, 1.0)
    top_ref[...] = top
    for i in range(4):
        stat_ref[i, 0:1] = jnp.where(some, top + jnp.log2(safe), MASK_VALUE)
        stat_ref[i, 1:2] = delta / safe


def second_kernel(q_ref, low_ref, high_ref, w_ref, d_ref, top_ref, stat_ref,
                  dq_ref, dk_ref, dv_ref, dq_acc):
    lse = [stat_ref[i, 0:1, :] for i in range(4)]
    top = jnp.maximum(jnp.maximum(lse[0], lse[1]), jnp.maximum(lse[2], lse[3]))
    share = [jnp.exp2(l - top) for l in lse]
    total = share[0] + share[1] + share[2] + share[3]
    delta = sum(share[i] * stat_ref[i, 1:2, :] for i in range(4)) / total
    factor = jnp.exp2(top_ref[0:1, :] - (top + jnp.log2(total)))
    queries, cotan = q_ref[:, 0:128], q_ref[:, 128:256]
    for s in range(N_K // K_STEP):
        rows = slice(s * K_STEP, (s + 1) * K_STEP)
        ref = low_ref if s < 2 else high_ref
        part = slice((s % 2) * K_STEP, (s % 2 + 1) * K_STEP)
        prob = w_ref[rows] * factor
        d_score = (prob * (d_ref[rows] - delta)).astype(BF)
        dv_ref[rows] = jnp.dot(prob.astype(BF), cotan, preferred_element_type=F32).astype(BF)
        dk_ref[rows] = jnp.dot(d_score, queries, preferred_element_type=F32)
        d_query = dot_tn(ref[part, 0:128], d_score)
        if s == 0:
            dq_acc[...] = d_query
        else:
            dq_acc[...] += d_query
    d_query = (dq_acc[...] * SCORE_SCALE).T.astype(BF)
    low = jnp.concatenate([low_ref[:, 256:384], high_ref[:, 256:384]], axis=0)
    high, rest = split(dot_tn(low, dv_ref[...]) * INV_RANK)
    for i in range(4):
        dq_ref[i, 0:256] = d_query[i * 256 : (i + 1) * 256]
        dq_ref[i, 256:288] = high[i * 32 : (i + 1) * 32]
        dq_ref[i, 288:320] = rest[i * 32 : (i + 1) * 32]


def scale_kernel(dk_ref, keep_ref, send_ref):
    core = lax.axis_index("core")
    for g in range(2):
        own = pl.ds(pl.multiple_of(g * 1024 + core * 512, 512), 512)
        other = pl.ds(pl.multiple_of(g * 1024 + (1 - core) * 512, 512), 512)
        keep_ref[g * 512 : (g + 1) * 512] = dk_ref[own] * SCORE_SCALE
        send_ref[g * 512 : (g + 1) * 512] = (dk_ref[other] * SCORE_SCALE).astype(BF)


def total_of(ref, rows):
    total = ref[0, rows].astype(F32)
    for i in range(1, 4):
        total = total + ref[i, rows].astype(F32)
    return total


def pair(value):
    high, rest = split(value)
    return jnp.concatenate([high.astype(F32), rest.astype(F32)], axis=0).astype(BF)


def x_sum_kernel(dq_ref, keep_ref, recv_ref, dq_out, out_ref):
    other = 1 - lax.axis_index("core")
    dq_out[...] = total_of(dq_ref, slice(0, 256)).astype(BF)
    grad = total_of(dq_ref, slice(256, 288)) + total_of(dq_ref, slice(288, 320))
    for y in range(4):
        at = slice(y * 256, (y + 1) * 256)
        out_ref[y, 0:256] = (keep_ref[at] + recv_ref[other, at].astype(F32)).astype(BF)
        out_ref[y, 256:272] = pair(grad[y * 8 : (y + 1) * 8])


def y_sum_kernel(dk_ref, dq_ref, out_ref):
    dk = total_of(dk_ref, slice(0, 256)).astype(BF)
    grad = total_of(dk_ref, slice(256, 272))
    grad = pair(grad[0:8] + grad[8:16])
    for z in range(4):
        rows = slice(z * HALF, (z + 1) * HALF)
        out_ref[z, 0:HALF, 0:128] = dq_ref[rows]
        out_ref[z, 0:HALF, 128:256] = dk[rows]
        out_ref[z, HALF : HALF + 16, 0:128] = grad
        out_ref[z, HALF : HALF + 16, 128:256] = jnp.zeros((16, 128), BF)


def last_kernel(back_ref, master_ref, first_ref, second_ref,
                qg_ref, kg_ref, nm_ref, nf_ref, ns_ref, tile_ref):
    z_hi, core = lax.axis_index("zh"), lax.axis_index("core")
    for half in range(2):
        for h in range(2):
            tile_ref[h, half * HALF : (half + 1) * HALF] = back_ref[half, core * 2 + h, 0:HALF, :]
    for out, lane in ((qg_ref, 0), (kg_ref, 128)):
        for h in range(2):
            out[h * HEAD : (h + 1) * HEAD, :] = tile_ref[h, :, lane : lane + LANES].T[0:HEAD]
    row8 = lax.broadcasted_iota(jnp.int32, (8, LANES), 0)
    columns = []
    for h in range(2):
        rows = (
            back_ref[0, core * 2 + h, HALF : HALF + 16, 0:128].astype(F32)
            + back_ref[1, core * 2 + h, HALF : HALF + 16, 0:128].astype(F32)
        )
        rows = rows[0:8] + rows[8:16]
        columns.append(jnp.concatenate(
            [
                jnp.sum(jnp.where(row8 == e * 4 + z_hi, rows, 0.0), axis=0, keepdims=True)
                for e in range(2)
            ],
            axis=0,
        )[:, 0:HEAD])
    gradient = jnp.concatenate(columns, axis=1)
    master = master_ref[...]
    new_first = BETA_ONE * first_ref[...] + (1.0 - BETA_ONE) * gradient
    new_second = BETA_TWO * second_ref[...] + (1.0 - BETA_TWO) * gradient * gradient
    direction = (
        new_first
        / (1.0 - BETA_ONE**STEP)
        / (jnp.sqrt(new_second / (1.0 - BETA_TWO**STEP)) + ADAM_EPSILON)
    )
    nm_ref[...] = master - LEARN_RATE * (direction + WEIGHT_DECAY * master)
    nf_ref[...] = new_first
    ns_ref[...] = new_second


def exchange(value, axes):
    return lax.all_to_all(value, axes, split_axis=0, concat_axis=0, tiled=True)


def swap(value):
    return lax.ppermute(value, "core", [(0, 1), (1, 0)])


def copies(value, count):
    return jnp.broadcast_to(value[None], (count, *value.shape)).reshape(
        count * value.shape[0], *value.shape[1:]
    )


def both_cores(value):
    return lax.all_gather(value, "core", axis=0)


def body(normed, w_down, query, key, value_base, cotangent, master, first, second):
    (part,) = call(low_kernel, [((TOK, RANK), F32)], (), (normed.T, w_down), limit=56)
    (part,) = call(half_kernel, [((4, HALF, RANK), F32)], (both_cores(part),))
    keep, send = call(
        pack_kernel,
        [((2, HALF, 512), BF), ((2, HALF, 512), BF)],
        (),
        (query.T, cotangent.T, key.T, value_base.T, master),
        [pltpu.VMEM((2, TOK, 512), BF), pltpu.VMEM((16, 256), F32)],
        limit=56,
    )
    part = exchange(part, "zl")
    recv = swap(send)
    (pieces,) = call(route_kernel, [((4, HALF, 640), BF)], (part, keep, recv))
    pieces = exchange(pieces, "zh").reshape(256, 640)
    k_own = exchange(copies(pieces[:, 256:640], 4), "y")
    (q_tile,) = call(mix_kernel, [((4, 256, 256), BF)], (pieces, k_own))
    k_low = both_cores(k_own[0:512]).reshape(1024, 384)
    k_high = both_cores(k_own[512:1024]).reshape(1024, 384)
    q_tile = exchange(q_tile, "x").reshape(N_Q, 256)

    stat, top, weight, d_prob = call(
        first_kernel,
        [((4, 2, N_Q), F32), ((1, N_Q), F32), ((N_K, N_Q), F32), ((N_K, N_Q), F32)],
        (q_tile, k_low, k_high),
        scratch=[pltpu.VMEM((N_K, LANES), BF)],
        limit=24,
    )
    stats = exchange(stat, "x")
    dq, dk = call(
        second_kernel,
        [((4, 320, LANES), BF), ((N_K, LANES), F32)],
        (q_tile, k_low, k_high, weight, d_prob, top, stats),
        scratch=[pltpu.VMEM((N_K, LANES), BF), pltpu.VMEM((LANES, N_Q), F32)],
        limit=16,
    )
    dk_keep, dk_send = call(
        scale_kernel, [((1024, LANES), F32), ((1024, LANES), BF)], (dk,)
    )
    dk_recv = both_cores(dk_send)
    dq, dk = call(
        x_sum_kernel,
        [((256, LANES), BF), ((4, 272, LANES), BF)],
        (exchange(dq, "x"), dk_keep, dk_recv),
    )
    (back,) = call(y_sum_kernel, [((4, HALF + 16, 256), BF)], (exchange(dk, "y"), dq))
    back = exchange(back, "zh")
    back = both_cores(back)
    q_grad, k_grad, new_master, new_first, new_second = call(
        last_kernel,
        [((2 * HEAD, TOK), BF)] * 2 + [((2, 2 * HEAD), F32)] * 3,
        (back,),
        (master, first, second),
        [pltpu.VMEM((2, TOK, 2 * LANES), BF)],
        pinned=False,
    )
    return q_grad.T, k_grad.T, new_master, new_first, new_second


def solution(mesh):
    fine = Mesh(mesh.devices.reshape(4, 4, 4, 4, 2), ("y", "zh", "x", "zl", "core"))
    seq, section = ("y", "zh", "x"), ("zl", "core")
    split = P(seq, section)
    return jax.shard_map(
        body,
        mesh=fine,
        in_specs=(split, P(section, None)) + (split,) * 7,
        out_specs=(split,) * 5,
        check_vma=False,
    )
```

```python
import math

import jax
import jax.numpy as jnp
from jax import lax
from jax.experimental import pallas as pl
from jax.experimental.pallas import tpu as pltpu
from jax.sharding import Mesh, PartitionSpec as P

HEAD = 112
LANES = 128
RANK = 128
STEP = 2

BETA_ONE = 0.9
BETA_TWO = 0.95
LEARN_RATE = 0.01
WEIGHT_DECAY = 0.1
ADAM_EPSILON = 1e-08
MASK_VALUE = -1e30
LOW_MAX = -1e20
SCORE_SCALE = 1.0 / math.sqrt(HEAD)
INV_RANK = 1.0 / math.sqrt(RANK)

BF = jnp.bfloat16
F32 = jnp.float32

TOK = 128
HALF = 64
N_Q = 1024
N_K = 2048
K_BLOCK = 256
K_STEP = 512
LOG2_E = math.log2(math.e)

VMEM = pl.BlockSpec(memory_space=pltpu.VMEM)


def call(kernel, shapes, args, outer=(), scratch=(), limit=8, pinned=True):
    return pl.pallas_call(
        kernel,
        out_shape=[(pltpu.VMEM if pinned else jax.ShapeDtypeStruct)(s, d) for s, d in shapes],
        in_specs=[VMEM] * (len(args) + len(outer)),
        out_specs=[VMEM] * len(shapes),
        scratch_shapes=list(scratch),
        compiler_params=pltpu.CompilerParams(vmem_limit_bytes=limit * 1024 * 1024),
    )(*[pltpu.with_memory_space_constraint(a, pltpu.VMEM) for a in args], *outer)


def dot_nt(a, b):
    return lax.dot_general(a, b, (((1,), (1,)), ((), ())), preferred_element_type=F32)


def dot_tn(a, b):
    return lax.dot_general(a, b, (((0,), (0,)), ((), ())), preferred_element_type=F32)


def rank_of(order):
    return (
        ((order >> 3) & 3) * 32 + (order & 3) * 8 + (order >> 5) * 2 + ((order >> 2) & 1)
    )


def iotas(rows, cols):
    return (
        lax.broadcasted_iota(jnp.int32, (rows, cols), 0),
        lax.broadcasted_iota(jnp.int32, (rows, cols), 1),
    )


def one_hot(mask):
    return jnp.where(mask, 1.0, 0.0).astype(BF)


def split(value):
    high = value.astype(BF)
    return high, (value - high.astype(F32)).astype(BF)


def half_kernel(part_ref, both_ref, out_ref):
    other = 1 - lax.axis_index("core")
    total = (
        part_ref[...]
        + both_ref[other, :, 1024:1152].astype(F32)
        + both_ref[other, :, 1152:1280].astype(F32)
    )
    for s in range(4):
        out_ref[s] = total


def pack_kernel(x_ref, wd_ref, q_ref, do_ref, k_ref, vb_ref, m_ref,
                part_ref, keep_ref, send_ref, full, w_pad, low):
    core = lax.axis_index("core")
    low[...] = dot_tn(x_ref[...], wd_ref[...])
    full[...] = jnp.zeros_like(full)
    for i, ref in enumerate((q_ref, do_ref, k_ref, vb_ref)):
        for h in range(2):
            tile = ref[h * HEAD : (h + 1) * HEAD, :].T
            full[h, :, i * LANES : i * LANES + HEAD] = tile
    w_pad[...] = jnp.zeros_like(w_pad)
    w_pad[0:2, 0 : 2 * HEAD] = m_ref[...]
    rows = w_pad[...].astype(BF)
    src, dst = iotas(16, LANES)
    for h in range(2):
        spread = sum(
            dot_tn(
                rows[:, h * HEAD + d * HALF : h * HEAD + (d + 1) * HALF],
                one_hot((src < 2) & (dst == HEAD + 2 * d + src)),
            )
            for d in range(2)
        ).astype(BF)
        for t in range(2):
            at = slice(t * HALF, (t + 1) * HALF)
            full[h, at, 384:512] = full[h, at, 384:512] + spread
    own = pl.ds(pl.multiple_of(core * HALF, HALF), HALF)
    other = pl.ds(pl.multiple_of((1 - core) * HALF, HALF), HALF)
    for h in range(2):
        keep_ref[h] = full[h, own, :]
        send_ref[:, h * 512 : (h + 1) * 512] = full[h, other, :]
    part_ref[...] = low[own, :]
    send_ref[:, 1024:1152], send_ref[:, 1152:1280] = split(low[other, :])


def route_kernel(part_ref, keep_ref, both_ref, out_ref):
    core = lax.axis_index("core")
    total = part_ref[0] + part_ref[1] + part_ref[2] + part_ref[3]
    src, dst = iotas(RANK, RANK)
    order = one_hot(src == rank_of(dst))
    low = jnp.dot(total.astype(BF), order, preferred_element_type=F32).astype(BF)
    for j in range(4):
        out_ref[j, :, 512:640] = low
    for h in range(2):
        out_ref[core * 2 + h, :, 0:512] = keep_ref[h]
        out_ref[(1 - core) * 2 + h, :, 0:512] = both_ref[1 - core, :, h * 512 : (h + 1) * 512]


def mix_kernel(piece_ref, k_ref, out_ref):
    lane = lax.broadcasted_iota(jnp.int32, (256, LANES), 1)
    here = (lane >= HEAD) & (lane < HEAD + 4)
    total = piece_ref[:, 0:128].astype(F32)
    for y in range(4):
        tile = k_ref[y * 256 : (y + 1) * 256, 128:256].astype(F32)
        tile = jnp.where(here, tile, 0.0)
        total = total + (pltpu.roll(tile, 4 * y, 1) if y else tile)
    total = total.astype(BF)
    for i in range(4):
        out_ref[i, :, 0:128] = total
        out_ref[i, :, 128:256] = piece_ref[:, 128:256]


def token_ids():
    y, x, core = lax.axis_index("y"), lax.axis_index("x"), lax.axis_index("core")
    n = lax.broadcasted_iota(jnp.int32, (1, N_Q), 1)
    q_tok = y * 2048 + ((n >> 6) & 3) * 512 + (n >> 8) * 128 + core * HALF + (n & 63)
    m = lax.broadcasted_iota(jnp.int32, (N_K, 1), 0)
    k_y, half = (m >> 10) * 2 + ((m >> 8) & 1), (m >> 9) & 1
    k_tok = k_y * 2048 + ((m >> 6) & 3) * 512 + x * 128 + half * HALF + (m & 63)
    return q_tok, k_tok


def fold(value, op):
    return op(value.reshape(value.shape[0] // 8, 8, value.shape[1]), axis=0)


def up_rows(q_ref):
    src, dst = iotas(LANES, RANK)
    lane = src - HEAD
    halves = []
    for d in range(2):
        place = one_hot(
            (lane >= 0) & (((lane >> 1) & 1) == d) & (dst == (lane & 1) * 4 + (lane >> 2) * 8)
        )
        spread = jnp.dot(q_ref[:, 0:128], place, preferred_element_type=F32)
        total = spread[0:HALF]
        for b in range(1, 16):
            tile = spread[b * HALF : (b + 1) * HALF]
            total = total + pltpu.roll(tile, (b >> 2) * 32 + (b & 3), 1)
        halves.append(total)
    return jnp.concatenate(halves, axis=0).astype(BF)


def first_kernel(q_ref, low_ref, high_ref, stat_ref, top_ref, w_ref, d_ref, v_ref):
    w_up = up_rows(q_ref)
    for h, ref in enumerate((low_ref, high_ref)):
        add = dot_nt(ref[:, 256:384], w_up) * INV_RANK
        v_ref[h * 1024 : (h + 1) * 1024] = (ref[:, 128:256].astype(F32) + add).astype(BF)
    q_tok, k_tok = token_ids()
    queries, cotan = q_ref[:, 0:128], q_ref[:, 128:256]
    highest = None
    for start in range(0, N_K, K_BLOCK):
        ref = low_ref if start < 1024 else high_ref
        part = slice(start % 1024, start % 1024 + K_BLOCK)
        rows = slice(start, start + K_BLOCK)
        scores = jnp.where(k_tok[rows] <= q_tok, dot_nt(ref[part, 0:128], queries), MASK_VALUE)
        w_ref[rows] = scores
        block = fold(scores, jnp.max)
        highest = block if highest is None else jnp.maximum(highest, block)
    scale = SCORE_SCALE * LOG2_E
    top = jnp.maximum(jnp.max(highest, axis=0, keepdims=True) * scale, LOW_MAX)
    total = delta = jnp.zeros((8, N_Q), F32)
    for start in range(0, N_K, K_BLOCK):
        rows = slice(start, start + K_BLOCK)
        weight = jnp.exp2(w_ref[rows] * scale - top)
        w_ref[rows] = weight
        d_prob = dot_nt(v_ref[rows], cotan)
        d_ref[rows] = d_prob
        total = total + fold(weight, jnp.sum)
        delta = delta + fold(weight * d_prob, jnp.sum)
    total = jnp.sum(total, axis=0, keepdims=True)
    delta = jnp.sum(delta, axis=0, keepdims=True)
    some = total > 0.0
    safe = jnp.where(some, total, 1.0)
    top_ref[...] = top
    for i in range(4):
        stat_ref[i, 0:1] = jnp.where(some, top + jnp.log2(safe), MASK_VALUE)
        stat_ref[i, 1:2] = delta / safe


def second_kernel(q_ref, low_ref, high_ref, w_ref, d_ref, top_ref, stat_ref,
                  dq_ref, dk_ref, dv_ref, dq_acc):
    lse = [stat_ref[i, 0:1, :] for i in range(4)]
    top = jnp.maximum(jnp.maximum(lse[0], lse[1]), jnp.maximum(lse[2], lse[3]))
    share = [jnp.exp2(l - top) for l in lse]
    total = share[0] + share[1] + share[2] + share[3]
    delta = sum(share[i] * stat_ref[i, 1:2, :] for i in range(4)) / total
    factor = jnp.exp2(top_ref[0:1, :] - (top + jnp.log2(total)))
    queries, cotan = q_ref[:, 0:128], q_ref[:, 128:256]
    for s in range(N_K // K_STEP):
        rows = slice(s * K_STEP, (s + 1) * K_STEP)
        ref = low_ref if s < 2 else high_ref
        part = slice((s % 2) * K_STEP, (s % 2 + 1) * K_STEP)
        prob = w_ref[rows] * factor
        d_score = (prob * (d_ref[rows] - delta)).astype(BF)
        dv_ref[rows] = jnp.dot(prob.astype(BF), cotan, preferred_element_type=F32).astype(BF)
        dk_ref[rows] = jnp.dot(d_score, queries, preferred_element_type=F32)
        d_query = dot_tn(ref[part, 0:128], d_score)
        if s == 0:
            dq_acc[...] = d_query
        else:
            dq_acc[...] += d_query
    d_query = (dq_acc[...] * SCORE_SCALE).T.astype(BF)
    low = jnp.concatenate([low_ref[:, 256:384], high_ref[:, 256:384]], axis=0)
    high, rest = split(dot_tn(low, dv_ref[...]) * INV_RANK)
    for i in range(4):
        dq_ref[i, 0:256] = d_query[i * 256 : (i + 1) * 256]
        dq_ref[i, 256:288] = high[i * 32 : (i + 1) * 32]
        dq_ref[i, 288:320] = rest[i * 32 : (i + 1) * 32]


def scale_kernel(dk_ref, keep_ref, send_ref):
    core = lax.axis_index("core")
    for g in range(2):
        own = pl.ds(pl.multiple_of(g * 1024 + core * 512, 512), 512)
        other = pl.ds(pl.multiple_of(g * 1024 + (1 - core) * 512, 512), 512)
        keep_ref[g * 512 : (g + 1) * 512] = dk_ref[own] * SCORE_SCALE
        send_ref[g * 512 : (g + 1) * 512] = (dk_ref[other] * SCORE_SCALE).astype(BF)


def total_of(ref, rows):
    total = ref[0, rows].astype(F32)
    for i in range(1, 4):
        total = total + ref[i, rows].astype(F32)
    return total


def pair(value):
    high, rest = split(value)
    return jnp.concatenate([high.astype(F32), rest.astype(F32)], axis=0).astype(BF)


def x_sum_kernel(dq_ref, keep_ref, recv_ref, dq_out, out_ref):
    other = 1 - lax.axis_index("core")
    dq_out[...] = total_of(dq_ref, slice(0, 256)).astype(BF)
    grad = total_of(dq_ref, slice(256, 288)) + total_of(dq_ref, slice(288, 320))
    for y in range(4):
        at = slice(y * 256, (y + 1) * 256)
        out_ref[y, 0:256] = (keep_ref[at] + recv_ref[other, at].astype(F32)).astype(BF)
        out_ref[y, 256:272] = pair(grad[y * 8 : (y + 1) * 8])


def free_lanes():
    src, dst = iotas(16, LANES)
    return one_hot(dst == HEAD + src)


def y_sum_kernel(dk_ref, dq_ref, out_ref):
    grad = total_of(dk_ref, slice(256, 272))
    grad = dot_tn(pair(grad[0:8] + grad[8:16]), free_lanes()).astype(BF)
    heads = lax.broadcasted_iota(jnp.int32, (256, LANES), 1) < HEAD
    dk = jnp.where(heads, total_of(dk_ref, slice(0, 256)), 0.0).astype(BF)
    dq = jnp.where(heads, dq_ref[...].astype(F32), 0.0).astype(BF)
    for z in range(4):
        rows = slice(z * HALF, (z + 1) * HALF)
        out_ref[z, :, 0:128] = dq[rows] + grad[0:HALF]
        out_ref[z, :, 128:256] = dk[rows] + grad[HALF:TOK]


def last_kernel(back_ref, master_ref, first_ref, second_ref,
                qg_ref, kg_ref, nm_ref, nf_ref, ns_ref, tile_ref):
    z_hi, core = lax.axis_index("zh"), lax.axis_index("core")
    for half in range(2):
        for h in range(2):
            tile_ref[h, half * HALF : (half + 1) * HALF] = back_ref[half, core * 2 + h]
    for out, lane in ((qg_ref, 0), (kg_ref, 128)):
        for h in range(2):
            out[h * HEAD : (h + 1) * HEAD, :] = tile_ref[h, :, lane : lane + LANES].T[0:HEAD]
    row8 = lax.broadcasted_iota(jnp.int32, (8, LANES), 0)
    columns = []
    for h in range(2):
        rows = sum(
            dot_nt(
                free_lanes(),
                jnp.concatenate(
                    [back_ref[i, core * 2 + h, :, 0:128], back_ref[i, core * 2 + h, :, 128:256]],
                    axis=0,
                ),
            )
            for i in range(2)
        )
        rows = rows[0:8] + rows[8:16]
        columns.append(jnp.concatenate(
            [
                jnp.sum(jnp.where(row8 == e * 4 + z_hi, rows, 0.0), axis=0, keepdims=True)
                for e in range(2)
            ],
            axis=0,
        )[:, 0:HEAD])
    gradient = jnp.concatenate(columns, axis=1)
    master = master_ref[...]
    new_first = BETA_ONE * first_ref[...] + (1.0 - BETA_ONE) * gradient
    new_second = BETA_TWO * second_ref[...] + (1.0 - BETA_TWO) * gradient * gradient
    direction = (
        new_first
        / (1.0 - BETA_ONE**STEP)
        / (jnp.sqrt(new_second / (1.0 - BETA_TWO**STEP)) + ADAM_EPSILON)
    )
    nm_ref[...] = master - LEARN_RATE * (direction + WEIGHT_DECAY * master)
    nf_ref[...] = new_first
    ns_ref[...] = new_second


def exchange(value, axes):
    return lax.all_to_all(value, axes, split_axis=0, concat_axis=0, tiled=True)


def copies(value, count):
    return jnp.broadcast_to(value[None], (count, *value.shape)).reshape(
        count * value.shape[0], *value.shape[1:]
    )


def both_cores(value):
    return lax.all_gather(value, "core", axis=0)


def body(normed, w_down, query, key, value_base, cotangent, master, first, second):
    part, keep, send = call(
        pack_kernel,
        [((HALF, RANK), F32), ((2, HALF, 512), BF), ((HALF, 1280), BF)],
        (),
        (normed.T, w_down, query.T, cotangent.T, key.T, value_base.T, master),
        [pltpu.VMEM((2, TOK, 512), BF), pltpu.VMEM((16, 256), F32), pltpu.VMEM((TOK, RANK), F32)],
        limit=56,
    )
    both = both_cores(send)
    (part,) = call(half_kernel, [((4, HALF, RANK), F32)], (part, both))
    part = exchange(part, "zl")
    (pieces,) = call(route_kernel, [((4, HALF, 640), BF)], (part, keep, both))
    pieces = exchange(pieces, "zh").reshape(256, 640)
    k_own = exchange(copies(pieces[:, 256:640], 4), "y")
    (q_tile,) = call(mix_kernel, [((4, 256, 256), BF)], (pieces, k_own))
    k_low = both_cores(k_own[0:512]).reshape(1024, 384)
    k_high = both_cores(k_own[512:1024]).reshape(1024, 384)
    q_tile = exchange(q_tile, "x").reshape(N_Q, 256)

    stat, top, weight, d_prob = call(
        first_kernel,
        [((4, 2, N_Q), F32), ((1, N_Q), F32), ((N_K, N_Q), F32), ((N_K, N_Q), F32)],
        (q_tile, k_low, k_high),
        scratch=[pltpu.VMEM((N_K, LANES), BF)],
        limit=24,
    )
    stats = exchange(stat, "x")
    dq, dk = call(
        second_kernel,
        [((4, 320, LANES), BF), ((N_K, LANES), F32)],
        (q_tile, k_low, k_high, weight, d_prob, top, stats),
        scratch=[pltpu.VMEM((N_K, LANES), BF), pltpu.VMEM((LANES, N_Q), F32)],
        limit=16,
    )
    dk_keep, dk_send = call(
        scale_kernel, [((1024, LANES), F32), ((1024, LANES), BF)], (dk,)
    )
    dk_recv = both_cores(dk_send)
    dq, dk = call(
        x_sum_kernel,
        [((256, LANES), BF), ((4, 272, LANES), BF)],
        (exchange(dq, "x"), dk_keep, dk_recv),
    )
    (back,) = call(y_sum_kernel, [((4, HALF, 256), BF)], (exchange(dk, "y"), dq))
    back = exchange(back, "zh")
    back = both_cores(back)
    q_grad, k_grad, new_master, new_first, new_second = call(
        last_kernel,
        [((2 * HEAD, TOK), BF)] * 2 + [((2, 2 * HEAD), F32)] * 3,
        (back,),
        (master, first, second),
        [pltpu.VMEM((2, TOK, 2 * LANES), BF)],
        pinned=False,
    )
    return q_grad.T, k_grad.T, new_master, new_first, new_second


def solution(mesh):
    fine = Mesh(mesh.devices.reshape(4, 4, 4, 4, 2), ("y", "zh", "x", "zl", "core"))
    seq, section = ("y", "zh", "x"), ("zl", "core")
    split = P(seq, section)
    return jax.shard_map(
        body,
        mesh=fine,
        in_specs=(split, P(section, None)) + (split,) * 7,
        out_specs=(split,) * 5,
        check_vma=False,
    )
```

```python
import math

import jax
import jax.numpy as jnp
from jax import lax
from jax.experimental import pallas as pl
from jax.experimental.pallas import tpu as pltpu
from jax.sharding import Mesh, PartitionSpec as P

HEAD = 112
LANES = 128
RANK = 128
STEP = 2

BETA_ONE = 0.9
BETA_TWO = 0.95
LEARN_RATE = 0.01
WEIGHT_DECAY = 0.1
ADAM_EPSILON = 1e-08
MASK_VALUE = -1e30
LOW_MAX = -1e20
SCORE_SCALE = 1.0 / math.sqrt(HEAD)
INV_RANK = 1.0 / math.sqrt(RANK)

BF = jnp.bfloat16
F32 = jnp.float32

TOK = 128
HALF = 64
N_Q = 1024
N_K = 2048
K_BLOCK = 256
K_STEP = 512
LOG2_E = math.log2(math.e)

VMEM = pl.BlockSpec(memory_space=pltpu.VMEM)


def call(kernel, shapes, args, outer=(), scratch=(), limit=8, pinned=True):
    return pl.pallas_call(
        kernel,
        out_shape=[(pltpu.VMEM if pinned else jax.ShapeDtypeStruct)(s, d) for s, d in shapes],
        in_specs=[VMEM] * (len(args) + len(outer)),
        out_specs=[VMEM] * len(shapes),
        scratch_shapes=list(scratch),
        compiler_params=pltpu.CompilerParams(vmem_limit_bytes=limit * 1024 * 1024),
    )(*[pltpu.with_memory_space_constraint(a, pltpu.VMEM) for a in args], *outer)


def dot_nt(a, b):
    return lax.dot_general(a, b, (((1,), (1,)), ((), ())), preferred_element_type=F32)


def dot_tn(a, b):
    return lax.dot_general(a, b, (((0,), (0,)), ((), ())), preferred_element_type=F32)


def rank_of(order):
    return (
        ((order >> 3) & 3) * 32 + (order & 3) * 8 + (order >> 5) * 2 + ((order >> 2) & 1)
    )


def iotas(rows, cols):
    return (
        lax.broadcasted_iota(jnp.int32, (rows, cols), 0),
        lax.broadcasted_iota(jnp.int32, (rows, cols), 1),
    )


def one_hot(mask):
    return jnp.where(mask, 1.0, 0.0).astype(BF)


def split(value):
    high = value.astype(BF)
    return high, (value - high.astype(F32)).astype(BF)


def half_kernel(part_ref, both_ref, out_ref):
    other = 1 - lax.axis_index("core")
    total = (
        part_ref[...]
        + both_ref[other, :, 1024:1152].astype(F32)
        + both_ref[other, :, 1152:1280].astype(F32)
    )
    for s in range(4):
        out_ref[s] = total


def pack_kernel(x_ref, wd_ref, q_ref, do_ref, k_ref, vb_ref, m_ref,
                part_ref, keep_ref, send_ref, full, w_pad, low):
    core = lax.axis_index("core")
    low[...] = dot_tn(x_ref[...], wd_ref[...])
    full[...] = jnp.zeros_like(full)
    for i, ref in enumerate((q_ref, do_ref, k_ref, vb_ref)):
        for h in range(2):
            tile = ref[h * HEAD : (h + 1) * HEAD, :].T
            full[h, :, i * LANES : i * LANES + HEAD] = tile
    w_pad[...] = jnp.zeros_like(w_pad)
    w_pad[0:2, 0 : 2 * HEAD] = m_ref[...]
    rows = w_pad[...].astype(BF)
    src, dst = iotas(16, LANES)
    for h in range(2):
        spread = sum(
            dot_tn(
                rows[:, h * HEAD + d * HALF : h * HEAD + (d + 1) * HALF],
                one_hot((src < 2) & (dst == HEAD + 2 * d + src)),
            )
            for d in range(2)
        ).astype(BF)
        for t in range(2):
            at = slice(t * HALF, (t + 1) * HALF)
            full[h, at, 384:512] = full[h, at, 384:512] + spread
    own = pl.ds(pl.multiple_of(core * HALF, HALF), HALF)
    other = pl.ds(pl.multiple_of((1 - core) * HALF, HALF), HALF)
    for h in range(2):
        keep_ref[h] = full[h, own, :]
        send_ref[:, h * 512 : (h + 1) * 512] = full[h, other, :]
    part_ref[...] = low[own, :]
    send_ref[:, 1024:1152], send_ref[:, 1152:1280] = split(low[other, :])


def route_kernel(part_ref, keep_ref, both_ref, out_ref):
    core = lax.axis_index("core")
    total = part_ref[0] + part_ref[1] + part_ref[2] + part_ref[3]
    src, dst = iotas(RANK, RANK)
    order = one_hot(src == rank_of(dst))
    low = jnp.dot(total.astype(BF), order, preferred_element_type=F32).astype(BF)
    for j in range(4):
        out_ref[j, :, 512:640] = low
    for h in range(2):
        out_ref[core * 2 + h, :, 0:512] = keep_ref[h]
        out_ref[(1 - core) * 2 + h, :, 0:512] = both_ref[1 - core, :, h * 512 : (h + 1) * 512]


def mix_kernel(piece_ref, k_ref, out_ref):
    lane = lax.broadcasted_iota(jnp.int32, (256, LANES), 1)
    here = (lane >= HEAD) & (lane < HEAD + 4)
    total = piece_ref[:, 0:128].astype(F32)
    for y in range(4):
        tile = k_ref[y * 256 : (y + 1) * 256, 128:256].astype(F32)
        tile = jnp.where(here, tile, 0.0)
        total = total + (pltpu.roll(tile, 4 * y, 1) if y else tile)
    total = total.astype(BF)
    for i in range(4):
        out_ref[i, :, 0:128] = total
        out_ref[i, :, 128:256] = piece_ref[:, 128:256]


def token_ids():
    y, x, core = lax.axis_index("y"), lax.axis_index("x"), lax.axis_index("core")
    n = lax.broadcasted_iota(jnp.int32, (1, N_Q), 1)
    q_tok = y * 2048 + ((n >> 6) & 3) * 512 + (n >> 8) * 128 + core * HALF + (n & 63)
    m = lax.broadcasted_iota(jnp.int32, (N_K, 1), 0)
    k_y, half = (m >> 10) * 2 + ((m >> 8) & 1), (m >> 9) & 1
    k_tok = k_y * 2048 + ((m >> 6) & 3) * 512 + x * 128 + half * HALF + (m & 63)
    return q_tok, k_tok


def fold(value, op):
    return op(value.reshape(value.shape[0] // 8, 8, value.shape[1]), axis=0)


def up_rows(q_ref):
    src, dst = iotas(LANES, RANK)
    lane = src - HEAD
    halves = []
    for d in range(2):
        place = one_hot(
            (lane >= 0) & (((lane >> 1) & 1) == d) & (dst == (lane & 1) * 4 + (lane >> 2) * 8)
        )
        spread = jnp.dot(q_ref[:, 0:128], place, preferred_element_type=F32)
        total = spread[0:HALF]
        for b in range(1, 16):
            tile = spread[b * HALF : (b + 1) * HALF]
            total = total + pltpu.roll(tile, (b >> 2) * 32 + (b & 3), 1)
        halves.append(total)
    return jnp.concatenate(halves, axis=0).astype(BF)


def first_kernel(q_ref, low_ref, high_ref, stat_ref, top_ref, w_ref, d_ref, v_ref):
    w_up = up_rows(q_ref)
    for h, ref in enumerate((low_ref, high_ref)):
        add = dot_nt(ref[:, 256:384], w_up) * INV_RANK
        v_ref[h * 1024 : (h + 1) * 1024] = (ref[:, 128:256].astype(F32) + add).astype(BF)
    q_tok, k_tok = token_ids()
    queries, cotan = q_ref[:, 0:128], q_ref[:, 128:256]
    highest = None
    for start in range(0, N_K, K_BLOCK):
        ref = low_ref if start < 1024 else high_ref
        part = slice(start % 1024, start % 1024 + K_BLOCK)
        rows = slice(start, start + K_BLOCK)
        scores = jnp.where(k_tok[rows] <= q_tok, dot_nt(ref[part, 0:128], queries), MASK_VALUE)
        w_ref[rows] = scores
        block = fold(scores, jnp.max)
        highest = block if highest is None else jnp.maximum(highest, block)
    scale = SCORE_SCALE * LOG2_E
    top = jnp.maximum(jnp.max(highest, axis=0, keepdims=True) * scale, LOW_MAX)
    total = delta = jnp.zeros((8, N_Q), F32)
    for start in range(0, N_K, K_BLOCK):
        rows = slice(start, start + K_BLOCK)
        weight = jnp.exp2(w_ref[rows] * scale - top)
        w_ref[rows] = weight
        d_prob = dot_nt(v_ref[rows], cotan)
        d_ref[rows] = d_prob
        total = total + fold(weight, jnp.sum)
        delta = delta + fold(weight * d_prob, jnp.sum)
    total = jnp.sum(total, axis=0, keepdims=True)
    delta = jnp.sum(delta, axis=0, keepdims=True)
    some = total > 0.0
    safe = jnp.where(some, total, 1.0)
    top_ref[...] = top
    for i in range(4):
        stat_ref[i, 0:1] = jnp.where(some, top + jnp.log2(safe), MASK_VALUE)
        stat_ref[i, 1:2] = delta / safe


def free_lanes():
    src, dst = iotas(16, LANES)
    return one_hot(dst == HEAD + src)


def second_kernel(q_ref, low_ref, high_ref, w_ref, d_ref, top_ref, stat_ref,
                  dq_ref, dk_ref, dv_ref, dq_acc):
    lse = [stat_ref[i, 0:1, :] for i in range(4)]
    top = jnp.maximum(jnp.maximum(lse[0], lse[1]), jnp.maximum(lse[2], lse[3]))
    share = [jnp.exp2(l - top) for l in lse]
    total = share[0] + share[1] + share[2] + share[3]
    delta = sum(share[i] * stat_ref[i, 1:2, :] for i in range(4)) / total
    factor = jnp.exp2(top_ref[0:1, :] - (top + jnp.log2(total)))
    queries, cotan = q_ref[:, 0:128], q_ref[:, 128:256]
    for s in range(N_K // K_STEP):
        rows = slice(s * K_STEP, (s + 1) * K_STEP)
        ref = low_ref if s < 2 else high_ref
        part = slice((s % 2) * K_STEP, (s % 2 + 1) * K_STEP)
        prob = w_ref[rows] * factor
        d_score = (prob * (d_ref[rows] - delta)).astype(BF)
        dv_ref[rows] = jnp.dot(prob.astype(BF), cotan, preferred_element_type=F32).astype(BF)
        dk_ref[rows] = jnp.dot(d_score, queries, preferred_element_type=F32)
        d_query = dot_tn(ref[part, 0:128], d_score)
        if s == 0:
            dq_acc[...] = d_query
        else:
            dq_acc[...] += d_query
    d_query = (dq_acc[...] * SCORE_SCALE).T.astype(BF)
    low = jnp.concatenate([low_ref[:, 256:384], high_ref[:, 256:384]], axis=0)
    high, rest = split(dot_tn(low, dv_ref[...]) * INV_RANK)
    for i in range(4):
        for j in range(2):
            start = i * 256 + j * TOK
            part = high[i * 32 + j * 16 : i * 32 + (j + 1) * 16]
            dq_ref[i, j * TOK : (j + 1) * TOK] = (
                d_query[start : start + TOK] + dot_tn(part, free_lanes()).astype(BF)
            )
        dq_ref[i, 256:288] = rest[i * 32 : (i + 1) * 32]


def scale_kernel(dk_ref, keep_ref, send_ref):
    core = lax.axis_index("core")
    for g in range(2):
        own = pl.ds(pl.multiple_of(g * 1024 + core * 512, 512), 512)
        other = pl.ds(pl.multiple_of(g * 1024 + (1 - core) * 512, 512), 512)
        keep_ref[g * 512 : (g + 1) * 512] = dk_ref[own] * SCORE_SCALE
        send_ref[g * 512 : (g + 1) * 512] = (dk_ref[other] * SCORE_SCALE).astype(BF)


def total_of(ref, rows):
    total = ref[0, rows].astype(F32)
    for i in range(1, 4):
        total = total + ref[i, rows].astype(F32)
    return total


def pair(value):
    high, rest = split(value)
    return jnp.concatenate([high.astype(F32), rest.astype(F32)], axis=0).astype(BF)


def x_sum_kernel(dq_ref, keep_ref, recv_ref, dq_out, out_ref):
    other = 1 - lax.axis_index("core")
    dq = total_of(dq_ref, slice(0, 256))
    dq_out[...] = dq.astype(BF)
    grad = total_of(dq_ref, slice(256, 288)) + jnp.concatenate(
        [dq[0:TOK].T[HEAD:LANES], dq[TOK:256].T[HEAD:LANES]], axis=0
    )
    heads = lax.broadcasted_iota(jnp.int32, (256, LANES), 1) < HEAD
    for y in range(4):
        at = slice(y * 256, (y + 1) * 256)
        dk = keep_ref[at] + recv_ref[other, at].astype(F32)
        dk = jnp.where(heads, dk, 0.0).astype(BF)
        placed = dot_tn(pair(grad[y * 8 : (y + 1) * 8]), free_lanes()).astype(BF)
        out_ref[y, 0:TOK] = dk[0:TOK] + placed
        out_ref[y, TOK:256] = dk[TOK:256]


def y_sum_kernel(dk_ref, dq_ref, out_ref):
    dk = total_of(dk_ref, slice(0, 256))
    grad = dk[0:TOK].T[HEAD:LANES]
    grad = dot_tn(pair(grad[0:8] + grad[8:16]), free_lanes()).astype(BF)
    heads = lax.broadcasted_iota(jnp.int32, (256, LANES), 1) < HEAD
    dk = jnp.where(heads, dk, 0.0).astype(BF)
    dq = jnp.where(heads, dq_ref[...].astype(F32), 0.0).astype(BF)
    for z in range(4):
        rows = slice(z * HALF, (z + 1) * HALF)
        out_ref[z, :, 0:128] = dq[rows] + grad[0:HALF]
        out_ref[z, :, 128:256] = dk[rows] + grad[HALF:TOK]


def last_kernel(back_ref, master_ref, first_ref, second_ref,
                qg_ref, kg_ref, nm_ref, nf_ref, ns_ref, tile_ref):
    z_hi, core = lax.axis_index("zh"), lax.axis_index("core")
    for half in range(2):
        for h in range(2):
            tile_ref[h, half * HALF : (half + 1) * HALF] = back_ref[half, core * 2 + h]
    for out, lane in ((qg_ref, 0), (kg_ref, 128)):
        for h in range(2):
            out[h * HEAD : (h + 1) * HEAD, :] = tile_ref[h, :, lane : lane + LANES].T[0:HEAD]
    row8 = lax.broadcasted_iota(jnp.int32, (8, LANES), 0)
    columns = []
    for h in range(2):
        rows = sum(
            dot_nt(
                free_lanes(),
                jnp.concatenate(
                    [back_ref[i, core * 2 + h, :, 0:128], back_ref[i, core * 2 + h, :, 128:256]],
                    axis=0,
                ),
            )
            for i in range(2)
        )
        rows = rows[0:8] + rows[8:16]
        columns.append(jnp.concatenate(
            [
                jnp.sum(jnp.where(row8 == e * 4 + z_hi, rows, 0.0), axis=0, keepdims=True)
                for e in range(2)
            ],
            axis=0,
        )[:, 0:HEAD])
    gradient = jnp.concatenate(columns, axis=1)
    master = master_ref[...]
    new_first = BETA_ONE * first_ref[...] + (1.0 - BETA_ONE) * gradient
    new_second = BETA_TWO * second_ref[...] + (1.0 - BETA_TWO) * gradient * gradient
    direction = (
        new_first
        / (1.0 - BETA_ONE**STEP)
        / (jnp.sqrt(new_second / (1.0 - BETA_TWO**STEP)) + ADAM_EPSILON)
    )
    nm_ref[...] = master - LEARN_RATE * (direction + WEIGHT_DECAY * master)
    nf_ref[...] = new_first
    ns_ref[...] = new_second


def exchange(value, axes):
    return lax.all_to_all(value, axes, split_axis=0, concat_axis=0, tiled=True)


def copies(value, count):
    return jnp.broadcast_to(value[None], (count, *value.shape)).reshape(
        count * value.shape[0], *value.shape[1:]
    )


def both_cores(value):
    return lax.all_gather(value, "core", axis=0)


def body(normed, w_down, query, key, value_base, cotangent, master, first, second):
    part, keep, send = call(
        pack_kernel,
        [((HALF, RANK), F32), ((2, HALF, 512), BF), ((HALF, 1280), BF)],
        (),
        (normed.T, w_down, query.T, cotangent.T, key.T, value_base.T, master),
        [pltpu.VMEM((2, TOK, 512), BF), pltpu.VMEM((16, 256), F32), pltpu.VMEM((TOK, RANK), F32)],
        limit=56,
    )
    both = both_cores(send)
    (part,) = call(half_kernel, [((4, HALF, RANK), F32)], (part, both))
    part = exchange(part, "zl")
    (pieces,) = call(route_kernel, [((4, HALF, 640), BF)], (part, keep, both))
    pieces = exchange(pieces, "zh").reshape(256, 640)
    k_own = exchange(copies(pieces[:, 256:640], 4), "y")
    (q_tile,) = call(mix_kernel, [((4, 256, 256), BF)], (pieces, k_own))
    k_low = both_cores(k_own[0:512]).reshape(1024, 384)
    k_high = both_cores(k_own[512:1024]).reshape(1024, 384)
    q_tile = exchange(q_tile, "x").reshape(N_Q, 256)

    stat, top, weight, d_prob = call(
        first_kernel,
        [((4, 2, N_Q), F32), ((1, N_Q), F32), ((N_K, N_Q), F32), ((N_K, N_Q), F32)],
        (q_tile, k_low, k_high),
        scratch=[pltpu.VMEM((N_K, LANES), BF)],
        limit=24,
    )
    stats = exchange(stat, "x")
    dq, dk = call(
        second_kernel,
        [((4, 288, LANES), BF), ((N_K, LANES), F32)],
        (q_tile, k_low, k_high, weight, d_prob, top, stats),
        scratch=[pltpu.VMEM((N_K, LANES), BF), pltpu.VMEM((LANES, N_Q), F32)],
        limit=16,
    )
    dk_keep, dk_send = call(
        scale_kernel, [((1024, LANES), F32), ((1024, LANES), BF)], (dk,)
    )
    dk_recv = both_cores(dk_send)
    dq, dk = call(
        x_sum_kernel,
        [((256, LANES), BF), ((4, 256, LANES), BF)],
        (exchange(dq, "x"), dk_keep, dk_recv),
    )
    (back,) = call(y_sum_kernel, [((4, HALF, 256), BF)], (exchange(dk, "y"), dq))
    back = exchange(back, "zh")
    back = both_cores(back)
    q_grad, k_grad, new_master, new_first, new_second = call(
        last_kernel,
        [((2 * HEAD, TOK), BF)] * 2 + [((2, 2 * HEAD), F32)] * 3,
        (back,),
        (master, first, second),
        [pltpu.VMEM((2, TOK, 2 * LANES), BF)],
        pinned=False,
    )
    return q_grad.T, k_grad.T, new_master, new_first, new_second


def solution(mesh):
    fine = Mesh(mesh.devices.reshape(4, 4, 4, 4, 2), ("y", "zh", "x", "zl", "core"))
    seq, section = ("y", "zh", "x"), ("zl", "core")
    split = P(seq, section)
    return jax.shard_map(
        body,
        mesh=fine,
        in_specs=(split, P(section, None)) + (split,) * 7,
        out_specs=(split,) * 5,
        check_vma=False,
    )
```

```python
import math

import jax
import jax.numpy as jnp
from jax import lax
from jax.experimental import pallas as pl
from jax.experimental.pallas import tpu as pltpu
from jax.sharding import Mesh, PartitionSpec as P

HEAD = 112
LANES = 128
RANK = 128
STEP = 2

BETA_ONE = 0.9
BETA_TWO = 0.95
LEARN_RATE = 0.01
WEIGHT_DECAY = 0.1
ADAM_EPSILON = 1e-08
MASK_VALUE = -1e30
LOW_MAX = -1e20
SCORE_SCALE = 1.0 / math.sqrt(HEAD)
INV_RANK = 1.0 / math.sqrt(RANK)

BF = jnp.bfloat16
F32 = jnp.float32

TOK = 128
HALF = 64
N_Q = 1024
N_K = 2048
K_BLOCK = 256
K_STEP = 512
LOG2_E = math.log2(math.e)

VMEM = pl.BlockSpec(memory_space=pltpu.VMEM)


def call(kernel, shapes, args, outer=(), scratch=(), limit=8, pinned=True):
    return pl.pallas_call(
        kernel,
        out_shape=[(pltpu.VMEM if pinned else jax.ShapeDtypeStruct)(s, d) for s, d in shapes],
        in_specs=[VMEM] * (len(args) + len(outer)),
        out_specs=[VMEM] * len(shapes),
        scratch_shapes=list(scratch),
        compiler_params=pltpu.CompilerParams(vmem_limit_bytes=limit * 1024 * 1024),
    )(*[pltpu.with_memory_space_constraint(a, pltpu.VMEM) for a in args], *outer)


def dot_nt(a, b):
    return lax.dot_general(a, b, (((1,), (1,)), ((), ())), preferred_element_type=F32)


def dot_tn(a, b):
    return lax.dot_general(a, b, (((0,), (0,)), ((), ())), preferred_element_type=F32)


def rank_of(order):
    return (
        ((order >> 3) & 3) * 32 + (order & 3) * 8 + (order >> 5) * 2 + ((order >> 2) & 1)
    )


def iotas(rows, cols):
    return (
        lax.broadcasted_iota(jnp.int32, (rows, cols), 0),
        lax.broadcasted_iota(jnp.int32, (rows, cols), 1),
    )


def one_hot(mask):
    return jnp.where(mask, 1.0, 0.0).astype(BF)


def split(value):
    high = value.astype(BF)
    return high, (value - high.astype(F32)).astype(BF)


def half_kernel(part_ref, both_ref, out_ref):
    other = 1 - lax.axis_index("core")
    total = (
        part_ref[...]
        + both_ref[other, :, 1024:1152].astype(F32)
        + both_ref[other, :, 1152:1280].astype(F32)
    )
    for s in range(4):
        out_ref[s] = total


def pack_kernel(x_ref, wd_ref, q_ref, do_ref, k_ref, vb_ref, m_ref,
                part_ref, keep_ref, send_ref, full, w_pad, low):
    core = lax.axis_index("core")
    low[...] = dot_tn(x_ref[...], wd_ref[...])
    full[...] = jnp.zeros_like(full)
    for i, ref in enumerate((q_ref, do_ref, k_ref, vb_ref)):
        for h in range(2):
            tile = ref[h * HEAD : (h + 1) * HEAD, :].T
            full[h, :, i * LANES : i * LANES + HEAD] = tile
    w_pad[...] = jnp.zeros_like(w_pad)
    w_pad[0:2, 0 : 2 * HEAD] = m_ref[...]
    rows = w_pad[...].astype(BF)
    src, dst = iotas(16, LANES)
    for h in range(2):
        spread = sum(
            dot_tn(
                rows[:, h * HEAD + d * HALF : h * HEAD + (d + 1) * HALF],
                one_hot((src < 2) & (dst == HEAD + 2 * d + src)),
            )
            for d in range(2)
        ).astype(BF)
        for t in range(2):
            at = slice(t * HALF, (t + 1) * HALF)
            full[h, at, 384:512] = full[h, at, 384:512] + spread
    own = pl.ds(pl.multiple_of(core * HALF, HALF), HALF)
    other = pl.ds(pl.multiple_of((1 - core) * HALF, HALF), HALF)
    for h in range(2):
        keep_ref[h] = full[h, own, :]
        send_ref[:, h * 512 : (h + 1) * 512] = full[h, other, :]
    part_ref[...] = low[own, :]
    send_ref[:, 1024:1152], send_ref[:, 1152:1280] = split(low[other, :])


def route_kernel(part_ref, keep_ref, both_ref, out_ref):
    core = lax.axis_index("core")
    total = part_ref[0] + part_ref[1] + part_ref[2] + part_ref[3]
    src, dst = iotas(RANK, RANK)
    order = one_hot(src == rank_of(dst))
    low = jnp.dot(total.astype(BF), order, preferred_element_type=F32).astype(BF)
    for j in range(4):
        out_ref[j, :, 512:640] = low
    for h in range(2):
        out_ref[core * 2 + h, :, 0:512] = keep_ref[h]
        out_ref[(1 - core) * 2 + h, :, 0:512] = both_ref[1 - core, :, h * 512 : (h + 1) * 512]


def mix_kernel(piece_ref, k_ref, out_ref):
    lane = lax.broadcasted_iota(jnp.int32, (256, LANES), 1)
    here = (lane >= HEAD) & (lane < HEAD + 4)
    total = piece_ref[:, 0:128].astype(F32)
    for y in range(4):
        tile = k_ref[y * 256 : (y + 1) * 256, 128:256].astype(F32)
        tile = jnp.where(here, tile, 0.0)
        total = total + (pltpu.roll(tile, 4 * y, 1) if y else tile)
    total = total.astype(BF)
    for i in range(4):
        out_ref[i, :, 0:128] = total
        out_ref[i, :, 128:256] = piece_ref[:, 128:256]


def token_ids():
    y, x, core = lax.axis_index("y"), lax.axis_index("x"), lax.axis_index("core")
    n = lax.broadcasted_iota(jnp.int32, (1, N_Q), 1)
    q_tok = y * 2048 + ((n >> 6) & 3) * 512 + (n >> 8) * 128 + core * HALF + (n & 63)
    m = lax.broadcasted_iota(jnp.int32, (N_K, 1), 0)
    k_y, half = (m >> 10) * 2 + ((m >> 8) & 1), (m >> 9) & 1
    k_tok = k_y * 2048 + ((m >> 6) & 3) * 512 + x * 128 + half * HALF + (m & 63)
    return q_tok, k_tok


def fold(value, op):
    return op(value.reshape(value.shape[0] // 8, 8, value.shape[1]), axis=0)


def up_rows(q_ref):
    src, dst = iotas(LANES, RANK)
    lane = src - HEAD
    halves = []
    for d in range(2):
        place = one_hot(
            (lane >= 0) & (((lane >> 1) & 1) == d) & (dst == (lane & 1) * 4 + (lane >> 2) * 8)
        )
        spread = jnp.dot(q_ref[:, 0:128], place, preferred_element_type=F32)
        total = spread[0:HALF]
        for b in range(1, 16):
            tile = spread[b * HALF : (b + 1) * HALF]
            total = total + pltpu.roll(tile, (b >> 2) * 32 + (b & 3), 1)
        halves.append(total)
    return jnp.concatenate(halves, axis=0).astype(BF)


def first_kernel(q_ref, low_ref, high_ref, stat_ref, top_ref, w_ref, d_ref, v_ref):
    w_up = up_rows(q_ref)
    for h, ref in enumerate((low_ref, high_ref)):
        add = dot_nt(ref[:, 256:384], w_up) * INV_RANK
        v_ref[h * 1024 : (h + 1) * 1024] = (ref[:, 128:256].astype(F32) + add).astype(BF)
    q_tok, k_tok = token_ids()
    queries, cotan = q_ref[:, 0:128], q_ref[:, 128:256]
    highest = None
    for start in range(0, N_K, K_BLOCK):
        ref = low_ref if start < 1024 else high_ref
        part = slice(start % 1024, start % 1024 + K_BLOCK)
        rows = slice(start, start + K_BLOCK)
        scores = jnp.where(k_tok[rows] <= q_tok, dot_nt(ref[part, 0:128], queries), MASK_VALUE)
        w_ref[rows] = scores
        block = fold(scores, jnp.max)
        highest = block if highest is None else jnp.maximum(highest, block)
    scale = SCORE_SCALE * LOG2_E
    top = jnp.maximum(jnp.max(highest, axis=0, keepdims=True) * scale, LOW_MAX)
    total = delta = jnp.zeros((8, N_Q), F32)
    for start in range(0, N_K, K_BLOCK):
        rows = slice(start, start + K_BLOCK)
        weight = jnp.exp2(w_ref[rows] * scale - top)
        w_ref[rows] = weight
        d_prob = dot_nt(v_ref[rows], cotan)
        d_ref[rows] = d_prob
        total = total + fold(weight, jnp.sum)
        delta = delta + fold(weight * d_prob, jnp.sum)
    total = jnp.sum(total, axis=0, keepdims=True)
    delta = jnp.sum(delta, axis=0, keepdims=True)
    some = total > 0.0
    safe = jnp.where(some, total, 1.0)
    top_ref[...] = top
    for i in range(4):
        stat_ref[i, 0:1] = jnp.where(some, top + jnp.log2(safe), MASK_VALUE)
        stat_ref[i, 1:2] = delta / safe


def free_lanes():
    src, dst = iotas(16, LANES)
    return one_hot(dst == HEAD + src)


def second_kernel(q_ref, low_ref, high_ref, w_ref, d_ref, top_ref, stat_ref,
                  dq_ref, dk_ref, dv_ref, dq_acc):
    lse = [stat_ref[i, 0:1, :] for i in range(4)]
    top = jnp.maximum(jnp.maximum(lse[0], lse[1]), jnp.maximum(lse[2], lse[3]))
    share = [jnp.exp2(l - top) for l in lse]
    total = share[0] + share[1] + share[2] + share[3]
    delta = sum(share[i] * stat_ref[i, 1:2, :] for i in range(4)) / total
    factor = jnp.exp2(top_ref[0:1, :] - (top + jnp.log2(total)))
    queries, cotan = q_ref[:, 0:128], q_ref[:, 128:256]
    for s in range(N_K // K_STEP):
        rows = slice(s * K_STEP, (s + 1) * K_STEP)
        ref = low_ref if s < 2 else high_ref
        part = slice((s % 2) * K_STEP, (s % 2 + 1) * K_STEP)
        prob = w_ref[rows] * factor
        d_score = (prob * (d_ref[rows] - delta)).astype(BF)
        dv_ref[rows] = jnp.dot(prob.astype(BF), cotan, preferred_element_type=F32).astype(BF)
        dk_ref[rows] = jnp.dot(d_score, queries, preferred_element_type=F32)
        d_query = dot_tn(ref[part, 0:128], d_score)
        if s == 0:
            dq_acc[...] = d_query
        else:
            dq_acc[...] += d_query
    d_query = (dq_acc[...] * SCORE_SCALE).T.astype(BF)
    low = jnp.concatenate([low_ref[:, 256:384], high_ref[:, 256:384]], axis=0)
    high, rest = split(dot_tn(low, dv_ref[...]) * INV_RANK)
    for i in range(4):
        for j in range(2):
            start = i * 256 + j * TOK
            part = high[i * 32 + j * 16 : i * 32 + (j + 1) * 16]
            dq_ref[i, j * TOK : (j + 1) * TOK] = (
                d_query[start : start + TOK] + dot_tn(part, free_lanes()).astype(BF)
            )
        dq_ref[i, 256:288] = rest[i * 32 : (i + 1) * 32]


def scale_kernel(dk_ref, keep_ref, send_ref):
    core = lax.axis_index("core")
    for g in range(2):
        own = pl.ds(pl.multiple_of(g * 1024 + core * 512, 512), 512)
        other = pl.ds(pl.multiple_of(g * 1024 + (1 - core) * 512, 512), 512)
        keep_ref[g * 512 : (g + 1) * 512] = dk_ref[own] * SCORE_SCALE
        send_ref[g * 512 : (g + 1) * 512] = (dk_ref[other] * SCORE_SCALE).astype(BF)


def total_of(ref, rows):
    total = ref[0, rows].astype(F32)
    for i in range(1, 4):
        total = total + ref[i, rows].astype(F32)
    return total


def pair(value):
    high, rest = split(value)
    return jnp.concatenate([high.astype(F32), rest.astype(F32)], axis=0).astype(BF)


def x_sum_kernel(dq_ref, keep_ref, recv_ref, dq_out, out_ref):
    other = 1 - lax.axis_index("core")
    dq = total_of(dq_ref, slice(0, 256))
    dq_out[...] = dq.astype(BF)
    grad = total_of(dq_ref, slice(256, 288)) + jnp.concatenate(
        [dq[0:TOK].T[HEAD:LANES], dq[TOK:256].T[HEAD:LANES]], axis=0
    )
    heads = lax.broadcasted_iota(jnp.int32, (256, LANES), 1) < HEAD
    for y in range(4):
        at = slice(y * 256, (y + 1) * 256)
        dk = keep_ref[at] + recv_ref[other, at].astype(F32)
        dk = jnp.where(heads, dk, 0.0).astype(BF)
        placed = dot_tn(pair(grad[y * 8 : (y + 1) * 8]), free_lanes()).astype(BF)
        out_ref[y, 0:TOK] = dk[0:TOK] + placed
        out_ref[y, TOK:256] = dk[TOK:256]


def y_sum_kernel(dk_ref, dq_ref, out_ref):
    dk = total_of(dk_ref, slice(0, 256))
    grad = dk[0:TOK].T[HEAD:LANES]
    grad = dot_tn(pair(grad[0:8] + grad[8:16]), free_lanes()).astype(BF)
    heads = lax.broadcasted_iota(jnp.int32, (256, LANES), 1) < HEAD
    dk = jnp.where(heads, dk, 0.0).astype(BF)
    dq = jnp.where(heads, dq_ref[...].astype(F32), 0.0).astype(BF)
    for z in range(4):
        rows = slice(z * HALF, (z + 1) * HALF)
        out_ref[z, :, 0:128] = dq[rows] + grad[0:HALF]
        out_ref[z, :, 128:256] = dk[rows] + grad[HALF:TOK]


def last_kernel(back_ref, master_ref, first_ref, second_ref,
                qg_ref, kg_ref, nm_ref, nf_ref, ns_ref, tile_ref):
    z_hi, core = lax.axis_index("zh"), lax.axis_index("core")
    for half in range(2):
        for h in range(2):
            tile_ref[h, half * HALF : (half + 1) * HALF] = back_ref[half, core * 2 + h]
    for out, lane in ((qg_ref, 0), (kg_ref, 128)):
        for h in range(2):
            out[h * HEAD : (h + 1) * HEAD, :] = tile_ref[h, :, lane : lane + LANES].T[0:HEAD]
    row8 = lax.broadcasted_iota(jnp.int32, (8, LANES), 0)
    columns = []
    for h in range(2):
        rows = sum(
            dot_nt(
                free_lanes(),
                jnp.concatenate(
                    [back_ref[i, core * 2 + h, :, 0:128], back_ref[i, core * 2 + h, :, 128:256]],
                    axis=0,
                ),
            )
            for i in range(2)
        )
        rows = rows[0:8] + rows[8:16]
        columns.append(jnp.concatenate(
            [
                jnp.sum(jnp.where(row8 == e * 4 + z_hi, rows, 0.0), axis=0, keepdims=True)
                for e in range(2)
            ],
            axis=0,
        )[:, 0:HEAD])
    gradient = jnp.concatenate(columns, axis=1)
    master = master_ref[...]
    new_first = BETA_ONE * first_ref[...] + (1.0 - BETA_ONE) * gradient
    new_second = BETA_TWO * second_ref[...] + (1.0 - BETA_TWO) * gradient * gradient
    direction = (
        new_first
        / (1.0 - BETA_ONE**STEP)
        / (jnp.sqrt(new_second / (1.0 - BETA_TWO**STEP)) + ADAM_EPSILON)
    )
    nm_ref[...] = master - LEARN_RATE * (direction + WEIGHT_DECAY * master)
    nf_ref[...] = new_first
    ns_ref[...] = new_second


def exchange(value, axes):
    return lax.all_to_all(value, axes, split_axis=0, concat_axis=0, tiled=True)


def both_cores(value):
    return lax.all_gather(value, "core", axis=0)


def body(normed, w_down, query, key, value_base, cotangent, master, first, second):
    part, keep, send = call(
        pack_kernel,
        [((HALF, RANK), F32), ((2, HALF, 512), BF), ((HALF, 1280), BF)],
        (),
        (normed.T, w_down, query.T, cotangent.T, key.T, value_base.T, master),
        [pltpu.VMEM((2, TOK, 512), BF), pltpu.VMEM((16, 256), F32), pltpu.VMEM((TOK, RANK), F32)],
        limit=56,
    )
    both = both_cores(send)
    (part,) = call(half_kernel, [((4, HALF, RANK), F32)], (part, both))
    part = exchange(part, "zl")
    (pieces,) = call(route_kernel, [((4, HALF, 640), BF)], (part, keep, both))
    pieces = exchange(pieces, "zh").reshape(256, 640)
    k_own = lax.all_gather(pieces[:, 256:640], "y", axis=0, tiled=True)
    (q_tile,) = call(mix_kernel, [((4, 256, 256), BF)], (pieces, k_own))
    k_low = both_cores(k_own[0:512]).reshape(1024, 384)
    k_high = both_cores(k_own[512:1024]).reshape(1024, 384)
    q_tile = exchange(q_tile, "x").reshape(N_Q, 256)

    stat, top, weight, d_prob = call(
        first_kernel,
        [((4, 2, N_Q), F32), ((1, N_Q), F32), ((N_K, N_Q), F32), ((N_K, N_Q), F32)],
        (q_tile, k_low, k_high),
        scratch=[pltpu.VMEM((N_K, LANES), BF)],
        limit=24,
    )
    stats = exchange(stat, "x")
    dq, dk = call(
        second_kernel,
        [((4, 288, LANES), BF), ((N_K, LANES), F32)],
        (q_tile, k_low, k_high, weight, d_prob, top, stats),
        scratch=[pltpu.VMEM((N_K, LANES), BF), pltpu.VMEM((LANES, N_Q), F32)],
        limit=16,
    )
    dk_keep, dk_send = call(
        scale_kernel, [((1024, LANES), F32), ((1024, LANES), BF)], (dk,)
    )
    dk_recv = both_cores(dk_send)
    dq, dk = call(
        x_sum_kernel,
        [((256, LANES), BF), ((4, 256, LANES), BF)],
        (exchange(dq, "x"), dk_keep, dk_recv),
    )
    (back,) = call(y_sum_kernel, [((4, HALF, 256), BF)], (exchange(dk, "y"), dq))
    back = exchange(back, "zh")
    back = both_cores(back)
    q_grad, k_grad, new_master, new_first, new_second = call(
        last_kernel,
        [((2 * HEAD, TOK), BF)] * 2 + [((2, 2 * HEAD), F32)] * 3,
        (back,),
        (master, first, second),
        [pltpu.VMEM((2, TOK, 2 * LANES), BF)],
        pinned=False,
    )
    return q_grad.T, k_grad.T, new_master, new_first, new_second


def solution(mesh):
    fine = Mesh(mesh.devices.reshape(4, 4, 4, 4, 2), ("y", "zh", "x", "zl", "core"))
    seq, section = ("y", "zh", "x"), ("zl", "core")
    split = P(seq, section)
    return jax.shard_map(
        body,
        mesh=fine,
        in_specs=(split, P(section, None)) + (split,) * 7,
        out_specs=(split,) * 5,
        check_vma=False,
    )
```
